256 devices in a mesh: dp: 16 (over z_lo, x), tensor: 16 (over z_hi, y, core).
Axes of the slice: x: 4, y: 4, z: 8 (z_hi: 2, z_lo: 4; z = z_hi * 4 + z_lo), core: 2. Of those that a mesh axis runs over, the one named last changes fastest.
Arguments:
- tokens: bfloat16 [8192, 8192], P('dp', 'tensor'), may hold values from -6 to 6
- cotangent: bfloat16 [8192, 8192], P('dp', 'tensor'), may hold values from -6 to 6
- w_first: bfloat16 [32, 256, 1024], P('tensor', 'dp'), may hold values from -0.375 to 0.375
- w_second: bfloat16 [128, 256, 256], P('tensor', 'dp'), may hold values from -0.375 to 0.375
- w_third: bfloat16 [128, 256, 256], P('tensor', 'dp'), may hold values from -0.375 to 0.375
- w_fourth: bfloat16 [32, 1024, 256], P('tensor', 'dp'), may hold values from -0.1875 to 0.1875
Outputs:
- layer_out: bfloat16 [8192, 8192], P('dp', 'tensor')
- grad_tokens: bfloat16 [8192, 8192], P('dp', 'tensor')
- grad_first: float32 [32, 256, 1024], P('tensor', 'dp')
- grad_second: float32 [128, 256, 256], P('tensor', 'dp')
- grad_third: float32 [128, 256, 256], P('tensor', 'dp')
- grad_fourth: float32 [32, 1024, 256], P('tensor', 'dp')
The draws below stay inside these ranges and needn't reach their ends.
All inputs are finite; a program needn't handle non-finite values.
Results may differ from the reference program's by a relative error of at most 0.0068.
Values may be sent and summed in bfloat16 or wider, within the bound.
No kernel may reach another device: no remote copies, remote signals or barrier semaphores. Data moves between devices by JAX's collectives and lax.ppermute only.
A program may use at most 64 MiB of HBM per device.

```python
import jax
import jax.numpy as jnp
from jax import lax

D = 8192
BS = 256
NA = 32
NJ = 128
RR = 8
TOKENS = 8192
N_DP = 16


def level_of(stream_key, shape, shards, smallest, largest):
    factor_of, own = 1.0, jax.random.fold_in(stream_key, 6)
    for position, shards_of in shards:
        draws = jnp.exp(jax.random.uniform(jax.random.fold_in(own, position), (shards_of,), jnp.float32, smallest / len(shards), largest / len(shards)))
        factor_of = factor_of * jnp.repeat(draws, shape[position] // shards_of).reshape([-1 if axis == position else 1 for axis in range(len(shape))])
    return factor_of


def gaussian(rng, dims, width, bound, split=(), kind=jnp.bfloat16):
    entries = width * jax.random.normal(rng, dims, jnp.float32)
    if split:
        entries = entries * level_of(rng, dims, split, -0.22, 0.18)
    return jnp.clip(entries, -bound, bound).astype(kind)


def setup_inputs(seed: int = 0) -> dict:
    arg_keys = jax.random.split(jax.random.key(seed), 7)
    return {
        "tokens": gaussian(arg_keys[0], (TOKENS, D), 1.0, 6.0, ((0, 16), (1, 16))),
        "cotangent": gaussian(arg_keys[1], (TOKENS, D), 1.0, 6.0, ((0, 16), (1, 16))),
        "w_first": gaussian(arg_keys[2], (NA, BS, NJ * RR), BS ** -0.5, 0.375, ((0, 16), (1, 16))),
        "w_second": gaussian(arg_keys[3], (NJ, NA * RR, BS), (NA * RR) ** -0.5, 0.375, ((0, 16), (1, 16))),
        "w_third": gaussian(arg_keys[4], (NJ, BS, NA * RR), BS ** -0.5, 0.375, ((0, 16), (1, 16))),
        "w_fourth": gaussian(arg_keys[5], (NA, NJ * RR, BS), (NJ * RR) ** -0.5, 0.1875, ((0, 16), (1, 16))),
    }


def rounded(values):
    return lax.optimization_barrier(values.astype(jnp.bfloat16)).astype(jnp.float32)

def gelu_tanh(values):
    return jax.nn.gelu(values, approximate=True)

def reference(tokens, cotangent, w_first, w_second, w_third, w_fourth):
    rows = TOKENS // N_DP
    first = w_first.astype(jnp.float32).reshape(NA, BS, NJ, RR)
    second = w_second.astype(jnp.float32).reshape(NJ, NA, RR, BS)
    third = w_third.astype(jnp.float32).reshape(NJ, BS, NA, RR)
    fourth = w_fourth.astype(jnp.float32).reshape(NA, NJ, RR, BS)

    def one_block(carry, pair):
        tok_block, cot_block = pair
        inputs = tok_block.astype(jnp.float32).reshape(rows, NA, BS)
        upstream = cot_block.astype(jnp.float32).reshape(rows, NA, BS)
        mid = rounded(jnp.einsum('tai,aijr->ajrt', inputs, first))
        pre = jnp.einsum('ajrt,jarc->jtc', mid, second)
        hidden = rounded(gelu_tanh(pre))
        back = rounded(jnp.einsum('jtc,jcar->ajrt', hidden, third))
        output = jnp.einsum('ajrt,ajro->tao', back, fourth).astype(jnp.bfloat16).reshape(rows, D)
        g_back = rounded(jnp.einsum('tao,ajro->ajrt', upstream, fourth))
        grad4 = jnp.einsum('ajrt,tao->ajro', back, upstream)
        g_hidden = jnp.einsum('ajrt,jcar->jtc', g_back, third)
        grad3 = jnp.einsum('jtc,ajrt->jcar', hidden, g_back)
        _, pull = jax.vjp(gelu_tanh, pre)
        g_pre = rounded(pull(g_hidden)[0])
        g_mid = rounded(jnp.einsum('jtc,jarc->ajrt', g_pre, second))
        grad2 = jnp.einsum('ajrt,jtc->jarc', mid, g_pre)
        g_input = jnp.einsum('ajrt,aijr->tai', g_mid, first).astype(jnp.bfloat16).reshape(rows, D)
        grad1 = jnp.einsum('tai,ajrt->aijr', inputs, g_mid)
        acc1, acc2, acc3, acc4 = carry
        return ((acc1 + grad1, acc2 + grad2, acc3 + grad3, acc4 + grad4), (output, g_input))
    start = (jnp.zeros((NA, BS, NJ, RR), jnp.float32), jnp.zeros((NJ, NA, RR, BS), jnp.float32), jnp.zeros((NJ, BS, NA, RR), jnp.float32), jnp.zeros((NA, NJ, RR, BS), jnp.float32))
    pairs = (tokens.reshape(N_DP, rows, D), cotangent.reshape(N_DP, rows, D))
    totals, (outputs, g_inputs) = lax.scan(one_block, start, pairs)
    grad1, grad2, grad3, grad4 = totals
    return (outputs.reshape(TOKENS, D), g_inputs.reshape(TOKENS, D), grad1.reshape(NA, BS, NJ * RR), grad2.reshape(NJ, NA * RR, BS), grad3.reshape(NJ, BS, NA * RR), grad4.reshape(NA, NJ * RR, BS))
```

```python
import jax
import jax.numpy as jnp
from jax import lax
from jax.experimental import pallas as pl
from jax.experimental.pallas import tpu as pltpu
from jax.sharding import Mesh
from jax.sharding import PartitionSpec as P

BS = 256
NA = 32
NJ = 128
RR = 8
AXES = ("zl", "x1", "x0", "zh", "y", "c")
WAYS = ("x1", "y", "c", "x0")
COPIES = ("zh", "zl")
bf16 = jnp.bfloat16
f32 = jnp.float32
C0 = 0.7978845608028654
C1 = 0.044715


def dot(a, b, ca, cb):
    return lax.dot_general(a, b, (((ca,), (cb,)), ((), ())), preferred_element_type=f32)


def call(kernel, grid, in_specs, out_specs, out_shape, flops, nbytes, trans=0):
    return pl.pallas_call(
        kernel,
        grid=grid,
        in_specs=in_specs,
        out_specs=out_specs,
        out_shape=out_shape,
        compiler_params=pltpu.CompilerParams(vmem_limit_bytes=48 * 1024 * 1024),
        cost_estimate=pl.CostEstimate(flops=flops, bytes_accessed=nbytes, transcendentals=trans),
    )


ONE = 2 * 1024 * 1024 * 256


def from_copies(block):
    return block.reshape(2, 4, 2, 16, BS).swapaxes(0, 1).reshape(BS, BS)


def to_copies(rows):
    return rows.reshape(4, 2, 2, 16, BS).swapaxes(0, 1)


def swap(pieces):
    x0 = lax.axis_index("x0")
    got = []
    for k in range(2):
        pairs = [
            (a * 4 + b * 2 + c, c * 4 + (b ^ k) * 2 + a)
            for a in range(2)
            for b in range(2)
            for c in range(2)
        ]
        piece = jnp.where((x0 ^ k) == 0, pieces[0], pieces[1])
        got.append(lax.ppermute(piece, ("x1", "x0", "zh"), pairs))
    first = x0 == 0
    return jnp.where(first, got[0], got[1]), jnp.where(first, got[1], got[0])


def mid_kernel(x_ref, w_ref, out_ref):
    w = from_copies(w_ref[...])
    out = dot(w.T, x_ref[...].reshape(1024, BS), 1, 1)
    out_ref[...] = out.astype(bf16).reshape(8, 32, 1024)


def g_back_kernel(g_ref, w_ref, out_ref):
    w = w_ref[...].reshape(BS, BS)
    out = dot(w, g_ref[...].reshape(1024, BS), 1, 1)
    out_ref[...] = out.astype(bf16).reshape(8, 32, 1024)


def group_rows(ref, k):
    rows = ref[...].astype(f32).reshape(NA, 2, RR, 1024)
    return rows[:, k].reshape(NA * RR, 1024).astype(bf16)


def both_groups(values):
    rows = [v.astype(bf16).astype(f32).reshape(NA, 1, RR, 1024) for v in values]
    return jnp.concatenate(rows, axis=1).reshape(NA, 2 * RR, 1024).astype(bf16)


def forward_kernel(mid_ref, w2_ref, w3_ref, back_ref):
    backs = []
    for k in range(2):
        mid = group_rows(mid_ref, k)
        second = from_copies(w2_ref[:, :, :, 0, k * 16 : (k + 1) * 16, :])
        third = from_copies(w3_ref[:, :, :, 0, k * 16 : (k + 1) * 16, :])
        pre = dot(second.T, mid, 1, 0)
        th = jnp.tanh(C0 * (pre + C1 * (pre * pre * pre)))
        hidden = (0.5 * pre * (1.0 + th)).astype(bf16)
        backs.append(dot(third.T, hidden, 1, 0))
    back_ref[...] = both_groups(backs)


def backward_kernel(mid_ref, gb_ref, w2_ref, w3_ref, gmid_ref, grad_ref):
    outs = []
    for k in range(2):
        rows = slice(k * 16, (k + 1) * 16)
        mid = group_rows(mid_ref, k)
        g_back = group_rows(gb_ref, k)
        second = from_copies(w2_ref[:, :, :, 0, rows, :])
        third = from_copies(w3_ref[:, :, :, 0, rows, :])
        pre = dot(second.T, mid, 1, 0)
        sq = pre * pre
        th = jnp.tanh(C0 * (pre + C1 * (sq * pre)))
        hidden = (0.5 * pre * (1.0 + th)).astype(bf16)
        slope = 0.5 * (1.0 + th) + 0.5 * pre * (1.0 - th * th) * (C0 * (1.0 + 3.0 * C1 * sq))
        g_pre = (dot(third, g_back, 1, 0) * slope).astype(bf16)
        outs.append(dot(second, g_pre, 1, 0))
        grad2 = dot(mid, g_pre, 1, 1)
        grad3 = dot(hidden, g_back, 1, 1)
        grad_ref[:, :, :, 0, rows, :] = to_copies(grad2.astype(bf16))
        grad_ref[:, :, :, 1, rows, :] = to_copies(grad3.astype(bf16))
    gmid_ref[...] = both_groups(outs)


def out_kernel(back_ref, g_ref, w_ref, out_ref, grad_ref, acc_ref):
    step = pl.program_id(0)
    back = back_ref[...].reshape(BS, 1024)
    w = w_ref[...].reshape(BS, BS)

    @pl.when(step == 0)
    def _():
        acc_ref[...] = jnp.zeros_like(acc_ref)

    acc_ref[...] += dot(w.T, back, 1, 0)
    grad = dot(back, g_ref[...].reshape(1024, BS), 1, 0)
    grad_ref[...] = grad.astype(bf16).reshape(grad_ref.shape)

    @pl.when(step == 3)
    def _():
        out_ref[...] = acc_ref[...].T.astype(bf16).reshape(2, 512, BS)


def in_kernel(gmid_ref, x_ref, w_ref, others_ref, out_ref, grad_ref, acc_ref):
    step = pl.program_id(0)
    gmid = gmid_ref[...].reshape(BS, 1024)
    w = from_copies(w_ref[...])

    @pl.when(step == 0)
    def _():
        acc_ref[...] = jnp.zeros_like(acc_ref)

    acc_ref[...] += dot(w, gmid, 1, 0)
    grad = dot(gmid, x_ref[...].reshape(1024, BS), 1, 0)
    grad_ref[...] = to_copies(grad.T.astype(bf16)).reshape(grad_ref.shape)

    @pl.when(step == 3)
    def _():
        out_ref[...] = acc_ref[...].T.astype(bf16).reshape(2, 512, BS)


S = jax.ShapeDtypeStruct
SPEC_T = pl.BlockSpec((2, 512, BS), lambda q: (0, 0, 0))
SPEC_R = pl.BlockSpec((8, 32, 1024), lambda q: (q, 0, 0))
SPEC_J = pl.BlockSpec((NA, 16, 1024), lambda q: (0, q, 0))


def spec_cols(f):
    return pl.BlockSpec((2, 4, 2, 1, 16, BS), lambda q: (0, 0, 0, f, q, 0))


def spec_rows(f):
    return pl.BlockSpec((2, 1, 2, 1, 64, BS), lambda q: (0, q, 0, f, 0, 0))


def spec_pair(f):
    return pl.BlockSpec((2, 4, 2, 1, 32, BS), lambda q: (0, 0, 0, f, q, 0))


ROWS = S((NA, 32, 1024), bf16)
TOKS = S((2, 512, BS), bf16)


def body(tokens, cotangent, w_first, w_second, w_third, w_fourth):
    first = w_first.reshape(2, 16, 4, BS).transpose(0, 2, 1, 3).reshape(2, 64, BS)
    second = w_second.reshape(2, 64, BS)
    third = w_third.reshape(2, 64, BS)
    w = jnp.stack([first, w_fourth, second, third], axis=1)
    w = jnp.stack(swap((w[0], w[1])))
    w14 = lax.all_gather(w[None, None, :, :2], COPIES, axis=0, tiled=True).reshape(2, 4, 2, 2, 64, BS)
    w23 = lax.all_gather(w[None, None, :, 2:], COPIES, axis=0, tiled=True).reshape(2, 4, 2, 2, 64, BS)
    acts = jnp.stack([tokens.reshape(512, 2, BS), cotangent.reshape(512, 2, BS)])
    first_half, second_half = swap((acts[:, :, 0], acts[:, :, 1]))
    x = jnp.stack([first_half[0], second_half[0]])
    g = jnp.stack([first_half[1], second_half[1]])

    mid = call(mid_kernel, (4,), [SPEC_T, spec_cols(0)], SPEC_R, ROWS, ONE, 3 << 20)(x, w14)
    mid = lax.all_to_all(mid, WAYS, 0, 0, tiled=True)
    g_back = call(g_back_kernel, (4,), [SPEC_T, spec_rows(1)], SPEC_R, ROWS, ONE, 3 << 20)(g, w14)
    g_back = lax.all_to_all(g_back, WAYS, 0, 0, tiled=True)
    back = call(
        forward_kernel, (2,), [SPEC_J, spec_pair(0), spec_pair(1)], SPEC_J, ROWS, 2 * ONE, 5 << 20, 1 << 20
    )(mid, w23, w23)
    back = lax.all_to_all(back, WAYS, 0, 0, tiled=True)
    g_mid, grad23 = call(
        backward_kernel,
        (2,),
        [SPEC_J, SPEC_J, spec_pair(0), spec_pair(1)],
        [SPEC_J, pl.BlockSpec((2, 4, 2, 2, 32, BS), lambda q: (0, 0, 0, 0, q, 0))],
        [ROWS, S((2, 4, 2, 2, 64, BS), bf16)],
        5 * ONE,
        8 << 20,
        1 << 20,
    )(mid, g_back, w23, w23)
    g_mid = lax.all_to_all(g_mid, WAYS, 0, 0, tiled=True)
    acc = pltpu.VMEM((BS, 1024), f32)
    params = pltpu.CompilerParams(vmem_limit_bytes=48 * 1024 * 1024)
    out, grad14 = pl.pallas_call(
        out_kernel,
        grid=(4,),
        in_specs=[SPEC_R, SPEC_T, spec_rows(1)],
        out_specs=[SPEC_T, spec_rows(1)],
        out_shape=[TOKS, S((2, 4, 2, 2, 64, BS), bf16)],
        scratch_shapes=[acc],
        compiler_params=params,
        cost_estimate=pl.CostEstimate(flops=2 * ONE, bytes_accessed=4 << 20, transcendentals=0),
    )(back, g, w14)
    g_in, grad14 = pl.pallas_call(
        in_kernel,
        grid=(4,),
        in_specs=[SPEC_R, SPEC_T, spec_cols(0), pl.BlockSpec(memory_space=pl.ANY)],
        out_specs=[SPEC_T, spec_cols(0)],
        out_shape=[TOKS, S((2, 4, 2, 2, 64, BS), bf16)],
        input_output_aliases={3: 1},
        scratch_shapes=[acc],
        compiler_params=params,
        cost_estimate=pl.CostEstimate(flops=2 * ONE, bytes_accessed=4 << 20, transcendentals=0),
    )(g_mid, x, w14, grad14)

    out = jnp.concatenate(swap((out[0], out[1])), axis=1)
    g_in = jnp.concatenate(swap((g_in[0], g_in[1])), axis=1)
    grad23 = grad23.reshape(8, 2, 2, 64, BS)
    grad14 = grad14.reshape(8, 2, 2, 64, BS)
    sum23 = lax.psum_scatter(grad23, COPIES, scatter_dimension=0, tiled=True)[0]
    sum14 = lax.psum_scatter(grad14, COPIES, scatter_dimension=0, tiled=True)[0]
    sum23 = jnp.stack(swap((sum23[0], sum23[1]))).astype(f32)
    sum14 = jnp.stack(swap((sum14[0], sum14[1]))).astype(f32)
    sum1 = sum14[:, 0].reshape(2, 4, 16, BS).transpose(0, 2, 1, 3).reshape(2, 16, 1024)
    return (
        out,
        g_in,
        sum1,
        sum23[:, 0].reshape(8, 16, BS),
        sum23[:, 1].reshape(8, 16, BS),
        sum14[:, 1],
    )


def solution(mesh):
    fine = Mesh(mesh.devices.reshape(4, 2, 2, 2, 4, 2), AXES)
    dp, tensor = ("zl", "x1", "x0"), ("zh", "y", "c")
    acts, weights = P(dp, tensor), P(tensor, dp, None)
    return jax.shard_map(
        body,
        mesh=fine,
        in_specs=(acts, acts, weights, weights, weights, weights),
        out_specs=(acts, acts, weights, weights, weights, weights),
        check_vma=False,
    )
```

```python
import jax
import jax.numpy as jnp
from jax import lax
from jax.experimental import pallas as pl
from jax.experimental.pallas import tpu as pltpu
from jax.sharding import Mesh
from jax.sharding import PartitionSpec as P

BS = 256
NA = 32
RR = 8
ROWS = 1024
AXES = ("zl", "x1", "x0", "zh", "y", "c")
WAYS = ("x1", "y", "c", "x0")
COPIES = ("zh", "zl")
SIDE = ("x1", "x0")
FAR = ("zl", "x1", "x0", "zh")
bf16 = jnp.bfloat16
f32 = jnp.float32
C0 = 0.7978845608028654
C1 = 0.044715
VMEM = 60 * 1024 * 1024
ONE = 2 * 1024 * 1024 * 256
S = jax.ShapeDtypeStruct


def dot(a, b, ca, cb):
    return lax.dot_general(a, b, (((ca,), (cb,)), ((), ())), preferred_element_type=f32)


def pack_kernel(zh_ref, x_ref, g_ref, first_ref, fourth_ref, out_ref):
    zh = zh_ref[0]
    for p in range(2):
        acts = jnp.where(zh == p, x_ref[...], g_ref[...])
        for b in range(2):
            first = jnp.concatenate([first_ref[b, :, q * BS : q * BS + BS] for q in range(4)], axis=0)
            rows = jnp.where(zh == p, first, fourth_ref[b])
            for t in range(2):
                out_ref[0, p, b, t, :64, :] = acts[t * 64 : t * 64 + 64, b * BS : b * BS + BS]
                out_ref[0, p, b, t, 64:, :] = rows


def up_kernel(x1_ref, x_ref, g_ref, first_ref, fourth_ref, out_ref):
    first = first_ref[...].reshape(BS, BS)
    mid = dot(first.T, x_ref[...].reshape(ROWS, BS), 1, 1).astype(bf16)
    g_back = dot(fourth_ref[...].reshape(BS, BS), g_ref[...].reshape(ROWS, BS), 1, 1).astype(bf16)
    for which, values in enumerate((mid, g_back)):
        values = values.reshape(2, 2, 2, 2, 16, ROWS)
        for a in range(2):
            out_ref[a, :, :, :, which, 0] = values[:, :, a]


def group_kernel(in_ref, w_ref, out_ref, grad_ref):
    def rows_of(which, m):
        rows = in_ref[:, which, 0].astype(f32).reshape(NA, 2, RR, ROWS)
        return rows[:, m].reshape(NA * RR, ROWS).astype(bf16)

    def both(values):
        rows = [v.astype(bf16).astype(f32).reshape(NA, 1, RR, ROWS) for v in values]
        return jnp.concatenate(rows, axis=1).reshape(NA, 2 * RR, ROWS).astype(bf16)

    def swapped(values):
        return jnp.concatenate([values[:, 128:], values[:, :128]], axis=1)

    backs, g_mids = [], []
    for m in range(2):
        second = w_ref[0, :, :, 0, m].reshape(BS, BS)
        third = swapped(w_ref[0, :, :, 1, m].reshape(BS, BS))
        mid = rows_of(0, m)
        g_back = rows_of(1, m)
        pre = dot(second.T, mid, 1, 0)
        sq = pre * pre
        th = jnp.tanh(C0 * (pre + C1 * (sq * pre)))
        hidden = (0.5 * pre * (1.0 + th)).astype(bf16)
        backs.append(dot(third.T, hidden, 1, 0))
        slope = 0.5 * (1.0 + th) + 0.5 * pre * (1.0 - th * th) * (C0 * (1.0 + 3.0 * C1 * sq))
        g_pre = (dot(third, g_back, 1, 0) * slope).astype(bf16)
        g_mids.append(dot(second, g_pre, 1, 0))
        grad_ref[0, :, :, 0, m] = dot(mid, g_pre, 1, 1).astype(bf16).reshape(4, 4, 16, BS)
        grad_ref[0, :, :, 1, m] = swapped(dot(hidden, g_back, 1, 1)).astype(bf16).reshape(4, 4, 16, BS)
    out_ref[:, 0, 0] = both(g_mids)
    out_ref[:, 1, 0] = both(backs)


def down_kernel(x1_ref, in_ref, x_ref, g_ref, first_ref, fourth_ref, out_ref, in_acc, out_acc):
    step = pl.program_id(0)
    x1 = x1_ref[0]
    g_mid, back = (
        jnp.stack([in_ref[a, :, :, :, which, 0] for a in range(2)], axis=2).reshape(BS, ROWS) for which in range(2)
    )
    g_in = dot(first_ref[...].reshape(BS, BS), g_mid, 1, 0)
    out = dot(fourth_ref[...].reshape(BS, BS).T, back, 1, 0)

    @pl.when(step == 0)
    def _():
        in_acc[...] = g_in
        out_acc[...] = out

    @pl.when(step > 0)
    def _():
        in_acc[...] += g_in
        out_acc[...] += out

    grad1 = dot(g_mid, x_ref[...].reshape(ROWS, BS), 1, 0)
    grad4 = dot(back, g_ref[...].reshape(ROWS, BS), 1, 0)
    at = pl.multiple_of(64 + step * 16, 16)
    out_ref[:, x1, pl.ds(at, 16), :] = grad1.T.astype(bf16).reshape(16, 16, BS)
    out_ref[pl.ds(step * 4, 4), 1 - x1, 64:, :] = grad4.astype(bf16).reshape(4, 64, BS)

    @pl.when(step == 3)
    def _():
        out_ref[:, x1, :64, :] = in_acc[...].T.astype(bf16).reshape(16, 64, BS)
        out_ref[:, 1 - x1, :64, :] = out_acc[...].T.astype(bf16).reshape(16, 64, BS)


def unpack_kernel(zh_ref, in_ref, out_side_ref, g_in_ref, out_ref, sum1_ref, sum4_ref):
    step = pl.program_id(0)

    @pl.when(step == 0)
    def _():
        sum1_ref[...] = jnp.zeros_like(sum1_ref)
        sum4_ref[...] = jnp.zeros_like(sum4_ref)

    for b in range(2):
        for t in range(2):
            g_in_ref[t * 64 : t * 64 + 64, b * BS : b * BS + BS] = in_ref[0, 0, b, t, :64, :]
            out_ref[t * 64 : t * 64 + 64, b * BS : b * BS + BS] = out_side_ref[0, 0, b, t, :64, :]
        grad1 = in_ref[0, 0, b, 0, 64:, :].astype(f32) + in_ref[0, 0, b, 1, 64:, :].astype(f32)
        for q in range(4):
            sum1_ref[b, :, q * BS : q * BS + BS] += grad1[q * 16 : q * 16 + 16]
        sum4_ref[b] += out_side_ref[0, 0, b, 0, 64:, :].astype(f32) + out_side_ref[0, 0, b, 1, 64:, :].astype(f32)


def call(kernel, grid, in_specs, out_specs, out_shape, flops, nbytes, trans=0, scratch=()):
    return pl.pallas_call(
        kernel,
        grid_spec=pltpu.PrefetchScalarGridSpec(
            num_scalar_prefetch=1,
            grid=grid,
            in_specs=in_specs,
            out_specs=out_specs,
            scratch_shapes=scratch,
        ),
        out_shape=out_shape,
        compiler_params=pltpu.CompilerParams(vmem_limit_bytes=VMEM),
        cost_estimate=pl.CostEstimate(flops=flops, bytes_accessed=nbytes, transcendentals=trans),
    )


SPEC_X = pl.BlockSpec((16, 1, 64, BS), lambda q, x1: (0, x1[0], 0, 0))
SPEC_G = pl.BlockSpec((16, 1, 64, BS), lambda q, x1: (0, 1 - x1[0], 0, 0))
SPEC_1 = pl.BlockSpec((16, 1, 16, BS), lambda q, x1: (0, x1[0], 4 + q, 0))
SPEC_4 = pl.BlockSpec((4, 1, 64, BS), lambda q, x1: (q, 1 - x1[0], 1, 0))
SPEC_Q = pl.BlockSpec((2, 2, 2, 2, 2, 1, 16, ROWS), lambda q, x1: (0, q % 2, 0, 0, 0, q // 2, 0, 0))
SPEC_J = pl.BlockSpec((NA, 2, 1, 16, ROWS), lambda k: (0, 0, k, 0, 0))
SPEC_W = pl.BlockSpec((1, 4, 4, 2, 2, 16, BS), lambda k: (k, 0, 0, 0, 0, 0, 0))
SPEC_T = pl.BlockSpec((128, 512), lambda z, zh: (z, 0))
WIRE = (2, 4, 2, 2, 2, 2, 16, ROWS)
PAIRS = (NA, 2, 2, 16, ROWS)


def body(tokens, cotangent, w_first, w_second, w_third, w_fourth):
    x1, zh = (lax.axis_index(n).astype(jnp.int32).reshape(1) for n in ("x1", "zh"))
    inner = jnp.stack([w_second.reshape(4, 2, 16, BS), w_third.reshape(4, 2, 16, BS)], axis=1)
    inner = lax.all_to_all(inner, SIDE, 0, 0, tiled=True)
    inner = lax.all_gather(inner[None], COPIES, axis=0, tiled=True).reshape(2, 4, 4, 2, 2, 16, BS)

    outer = call(
        pack_kernel,
        (4,),
        [
            SPEC_T,
            SPEC_T,
            pl.BlockSpec((2, 16, 1024), lambda z, zh: (0, 0, 0)),
            pl.BlockSpec((2, 64, BS), lambda z, zh: (0, 0, 0)),
        ],
        pl.BlockSpec((1, 2, 2, 2, 128, BS), lambda z, zh: (z, 0, 0, 0, 0, 0)),
        S((4, 2, 2, 2, 128, BS), bf16),
        0,
        3 << 20,
    )(zh, tokens, cotangent, w_first, w_fourth)
    outer = lax.all_to_all(outer.reshape(32, 128, BS), FAR, 0, 0, tiled=True).reshape(16, 2, 128, BS)

    wire = call(up_kernel, (4,), [SPEC_X, SPEC_G, SPEC_1, SPEC_4], SPEC_Q, S(WIRE, bf16), 2 * ONE, 6 << 20)(
        x1, outer, outer, outer, outer
    )
    wire = lax.all_to_all(wire.reshape(PAIRS), WAYS, 0, 0, tiled=True)
    wire, grads = pl.pallas_call(
        group_kernel,
        grid=(2,),
        in_specs=[SPEC_J, SPEC_W],
        out_specs=[SPEC_J, SPEC_W],
        out_shape=[S(PAIRS, bf16), S((2, 4, 4, 2, 2, 16, BS), bf16)],
        compiler_params=pltpu.CompilerParams(vmem_limit_bytes=VMEM),
        cost_estimate=pl.CostEstimate(flops=6 * ONE, bytes_accessed=10 << 20, transcendentals=1 << 20),
    )(wire, inner)
    wire = lax.all_to_all(wire, WAYS, 0, 0, tiled=True)
    sums = lax.psum_scatter(grads.reshape(8, 4, 2, 2, 16, BS), COPIES, scatter_dimension=0, tiled=True)[0]
    sums = lax.all_to_all(sums, SIDE, 0, 0, tiled=True)

    acc = pltpu.VMEM((BS, ROWS), f32)
    outer = call(
        down_kernel,
        (4,),
        [SPEC_Q, SPEC_X, SPEC_G, SPEC_1, SPEC_4],
        pl.BlockSpec((16, 2, 128, BS), lambda q, x1: (0, 0, 0, 0)),
        S((16, 2, 128, BS), bf16),
        4 * ONE,
        8 << 20,
        scratch=[acc, acc],
    )(x1, wire.reshape(WIRE), outer, outer, outer, outer)

    outer = lax.all_to_all(outer.reshape(32, 128, BS), FAR, 0, 0, tiled=True).reshape(4, 2, 2, 2, 128, BS)
    g_in, out, sum1, sum4 = call(
        unpack_kernel,
        (4,),
        [
            pl.BlockSpec((1, 1, 2, 2, 128, BS), lambda z, zh: (z, zh[0], 0, 0, 0, 0)),
            pl.BlockSpec((1, 1, 2, 2, 128, BS), lambda z, zh: (z, 1 - zh[0], 0, 0, 0, 0)),
        ],
        [
            SPEC_T,
            SPEC_T,
            pl.BlockSpec((2, 16, 1024), lambda z, zh: (0, 0, 0)),
            pl.BlockSpec((2, 64, BS), lambda z, zh: (0, 0, 0)),
        ],
        [S((512, 512), bf16), S((512, 512), bf16), S((2, 16, 1024), f32), S((2, 64, BS), f32)],
        1 << 20,
        4 << 20,
    )(zh, outer, outer)
    sum2, sum3 = (sums[:, f].reshape(8, 16, BS).astype(f32) for f in range(2))
    return out, g_in, sum1, sum2, sum3, sum4


def solution(mesh):
    fine = Mesh(mesh.devices.reshape(4, 2, 2, 2, 4, 2), AXES)
    dp, tensor = ("zl", "x1", "x0"), ("zh", "y", "c")
    acts, weights = P(dp, tensor), P(tensor, dp, None)
    return jax.shard_map(
        body,
        mesh=fine,
        in_specs=(acts, acts, weights, weights, weights, weights),
        out_specs=(acts, acts, weights, weights, weights, weights),
        check_vma=False,
    )
```

```python
import jax
import jax.numpy as jnp
from jax import lax
from jax.experimental import pallas as pl
from jax.experimental.pallas import tpu as pltpu
from jax.sharding import Mesh
from jax.sharding import PartitionSpec as P

BS = 256
NA = 32
RR = 8
ROWS = 1024
HALF = 512
AXES = ("zl", "x1", "x0", "zh", "y", "c")
WAYS = ("x1", "y", "c", "x0")
COPIES = ("zh", "zl")
SIDE = ("x1", "x0")
FAR = ("zl", "x1", "x0", "zh")
bf16 = jnp.bfloat16
f32 = jnp.float32
C0 = 0.7978845608028654
C1 = 0.044715
VMEM = 60 * 1024 * 1024
ONE = 2 * 1024 * 1024 * 256
S = jax.ShapeDtypeStruct


def dot(a, b, ca, cb):
    return lax.dot_general(a, b, (((ca,), (cb,)), ((), ())), preferred_element_type=f32)


def pack_weights_kernel(zh_ref, first_ref, second_ref, third_ref, fourth_ref, out_ref):
    zh = zh_ref[0]
    for p in range(2):
        for b in range(2):
            x = 2 * p + b
            first = jnp.concatenate([first_ref[b, :, q * BS : q * BS + BS] for q in range(4)], axis=0)
            out_ref[x, :64] = jnp.where(zh == p, first, fourth_ref[b])
            for m in range(2):
                out_ref[x, 64 + m * 16 : 80 + m * 16] = second_ref[2 * x + m]
                out_ref[x, 96 + m * 16 : 112 + m * 16] = third_ref[2 * x + m]


def unpack_weights_kernel(zh_ref, in_ref, sum1_ref, sum2_ref, sum3_ref, sum4_ref):
    zh = zh_ref[0]
    for b in range(2):
        low, high = in_ref[b, :64].astype(f32), in_ref[2 + b, :64].astype(f32)
        first = jnp.where(zh == 0, low, high)
        for q in range(4):
            sum1_ref[b, :, q * BS : q * BS + BS] = first[q * 16 : q * 16 + 16]
        sum4_ref[b] = jnp.where(zh == 0, high, low)
    for x in range(4):
        for m in range(2):
            sum2_ref[2 * x + m] = in_ref[x, 64 + m * 16 : 80 + m * 16].astype(f32)
            sum3_ref[2 * x + m] = in_ref[x, 96 + m * 16 : 112 + m * 16].astype(f32)


def pack_kernel(zh_ref, x_ref, g_ref, out_ref):
    zh = zh_ref[0]
    for p in range(2):
        acts = jnp.where(zh == p, x_ref[...], g_ref[...])
        for b in range(2):
            for t in range(2):
                out_ref[0, p, b, t] = acts[t * 64 : t * 64 + 64, b * BS : b * BS + BS]


def unpack_kernel(zh_ref, in_ref, out_side_ref, g_in_ref, out_ref):
    for b in range(2):
        for t in range(2):
            g_in_ref[t * 64 : t * 64 + 64, b * BS : b * BS + BS] = in_ref[0, 0, b, t]
            out_ref[t * 64 : t * 64 + 64, b * BS : b * BS + BS] = out_side_ref[0, 0, b, t]


def up_kernel(x1_ref, x_ref, g_ref, first_ref, fourth_ref, out_ref):
    first = first_ref[...].reshape(16, 4, 16, BS)
    first = jnp.concatenate([first[:, q].reshape(BS, BS).T for q in range(4)], axis=0)
    mid = dot(first, x_ref[...].reshape(HALF, BS), 1, 1).astype(bf16)
    g_back = dot(fourth_ref[...].reshape(ROWS, BS), g_ref[...].reshape(HALF, BS), 1, 1).astype(bf16)
    for which, values in enumerate((mid, g_back)):
        values = values.reshape(2, 4, 2, 2, 2, 16, HALF)
        for k in range(2):
            for a in range(2):
                out_ref[a, :, :, :, which, k] = values[k, :, :, a]


def group_kernel(in_ref, w_ref, out_ref, grad_ref):
    def rows_of(which, m):
        rows = in_ref[:, which, 0].astype(f32).reshape(NA, 2, RR, ROWS)
        return rows[:, m].reshape(NA * RR, ROWS).astype(bf16)

    def both(values):
        rows = [v.astype(bf16).astype(f32).reshape(NA, 1, RR, ROWS) for v in values]
        return jnp.concatenate(rows, axis=1).reshape(NA, 2 * RR, ROWS).astype(bf16)

    def swapped(values):
        return jnp.concatenate([values[:, 128:], values[:, :128]], axis=1)

    backs, g_mids = [], []
    for m in range(2):
        second = w_ref[0, :, :, m * 16 : m * 16 + 16].reshape(BS, BS)
        third = swapped(w_ref[0, :, :, 32 + m * 16 : 48 + m * 16].reshape(BS, BS))
        mid = rows_of(0, m)
        g_back = rows_of(1, m)
        pre = dot(second.T, mid, 1, 0)
        sq = pre * pre
        th = jnp.tanh(pre * (C0 + (C0 * C1) * sq))
        half = 0.5 * pre
        part = half * th
        hidden = (half + part).astype(bf16)
        backs.append(dot(third.T, hidden, 1, 0))
        slope = (0.5 + 0.5 * th) + (half - part * th) * (C0 + (3.0 * C0 * C1) * sq)
        g_pre = (dot(third, g_back, 1, 0) * slope).astype(bf16)
        g_mids.append(dot(second, g_pre, 1, 0))
        grad_ref[0, :, :, m * 16 : m * 16 + 16] = dot(mid, g_pre, 1, 1).astype(bf16).reshape(4, 4, 16, BS)
        grad3 = swapped(dot(hidden, g_back, 1, 1)).astype(bf16)
        grad_ref[0, :, :, 32 + m * 16 : 48 + m * 16] = grad3.reshape(4, 4, 16, BS)
    out_ref[:, 0, 0] = both(g_mids)
    out_ref[:, 1, 0] = both(backs)


def down_kernel(x1_ref, in_ref, x_ref, g_ref, first_ref, fourth_ref, out_ref, grad_ref, acc1, acc4):
    step = pl.program_id(0)
    x1 = x1_ref[0]
    g_mid, back = (
        jnp.stack(
            [jnp.stack([in_ref[a, :, :, :, which, k] for a in range(2)], axis=2) for k in range(2)], axis=0
        ).reshape(ROWS, HALF)
        for which in range(2)
    )
    first = first_ref[...].reshape(16, 4, 16, BS)
    first = jnp.concatenate([first[:, q].reshape(BS, BS) for q in range(4)], axis=1)
    g_in = dot(first, g_mid, 1, 0)
    out = dot(fourth_ref[...].reshape(ROWS, BS).T, back, 1, 0)
    out_ref[:, x1] = g_in.T.astype(bf16).reshape(8, 64, BS)
    out_ref[:, 1 - x1] = out.T.astype(bf16).reshape(8, 64, BS)
    grad1 = dot(g_mid, x_ref[...].reshape(HALF, BS), 1, 0)
    grad4 = dot(back, g_ref[...].reshape(HALF, BS), 1, 0)

    @pl.when(step == 0)
    def _():
        acc1[...] = grad1
        acc4[...] = grad4

    @pl.when(step == 1)
    def _():
        for q in range(4):
            rows = slice(q * BS, q * BS + BS)
            grad = (acc1[rows] + grad1[rows]).T.astype(bf16)
            grad_ref[x1, :, :, q * 16 : q * 16 + 16, :] = grad.reshape(4, 4, 16, BS)
        grad_ref[1 - x1] = (acc4[...] + grad4).astype(bf16).reshape(4, 4, 64, BS)


def call(kernel, grid, in_specs, out_specs, out_shape, flops, nbytes, trans=0, scratch=()):
    return pl.pallas_call(
        kernel,
        grid_spec=pltpu.PrefetchScalarGridSpec(
            num_scalar_prefetch=1,
            grid=grid,
            in_specs=in_specs,
            out_specs=out_specs,
            scratch_shapes=scratch,
        ),
        out_shape=out_shape,
        compiler_params=pltpu.CompilerParams(vmem_limit_bytes=VMEM),
        cost_estimate=pl.CostEstimate(flops=flops, bytes_accessed=nbytes, transcendentals=trans),
    )


SPEC_X = pl.BlockSpec((8, 1, 64, BS), lambda t, x1: (t, x1[0], 0, 0))
SPEC_G = pl.BlockSpec((8, 1, 64, BS), lambda t, x1: (t, 1 - x1[0], 0, 0))
SPEC_1 = pl.BlockSpec((1, 4, 4, 64, BS), lambda t, x1: (x1[0], 0, 0, 0, 0))
SPEC_4 = pl.BlockSpec((1, 4, 4, 64, BS), lambda t, x1: (1 - x1[0], 0, 0, 0, 0))
SPEC_Q = pl.BlockSpec((2, 4, 2, 2, 2, 2, 16, HALF), lambda t, x1: (0, 0, 0, 0, 0, 0, 0, t))
SPEC_J = pl.BlockSpec((NA, 2, 1, 16, ROWS), lambda k: (0, 0, k, 0, 0))
SPEC_W = pl.BlockSpec((1, 4, 4, 64, BS), lambda k: (k, 0, 0, 1, 0))
SPEC_GRAD = pl.BlockSpec((1, 4, 4, 64, BS), lambda k: (k, 0, 0, 0, 0))
SPEC_T = pl.BlockSpec((128, 512), lambda z, zh: (z, 0))
WIRE = (2, 4, 2, 2, 2, 2, 16, ROWS)
PAIRS = (NA, 2, 2, 16, ROWS)


def whole(shape):
    return pl.BlockSpec(shape, lambda *_: (0,) * len(shape))


FACTORS = [S((2, 16, 1024), f32), S((8, 16, BS), f32), S((8, 16, BS), f32), S((2, 64, BS), f32)]
SPEC_FACTORS = [whole(factor.shape) for factor in FACTORS]
SLOTS = (4, 2, 2, 2, 64, BS)


def body(tokens, cotangent, w_first, w_second, w_third, w_fourth):
    x1, zh = (lax.axis_index(n).astype(jnp.int32).reshape(1) for n in ("x1", "zh"))
    w = call(pack_weights_kernel, (1,), SPEC_FACTORS, whole((4, 128, BS)), S((4, 128, BS), bf16), 0, 1 << 19)(
        zh, w_first, w_second, w_third, w_fourth
    )
    w = lax.all_to_all(w, SIDE, 0, 0, tiled=True)
    acts = call(
        pack_kernel,
        (4,),
        [SPEC_T, SPEC_T],
        pl.BlockSpec((1, 2, 2, 2, 64, BS), lambda z, zh: (z, 0, 0, 0, 0, 0)),
        S(SLOTS, bf16),
        0,
        2 << 20,
    )(zh, tokens, cotangent)
    w, acts = lax.optimization_barrier((w, acts))
    w = lax.all_gather(w[None], COPIES, axis=0, tiled=True).reshape(2, 4, 4, 128, BS)
    acts = lax.all_to_all(acts.reshape(32, 64, BS), FAR, 0, 0, tiled=True).reshape(16, 2, 64, BS)

    wire = call(up_kernel, (2,), [SPEC_X, SPEC_G, SPEC_1, SPEC_4], SPEC_Q, S(WIRE, bf16), 2 * ONE, 6 << 20)(
        x1, acts, acts, w, w
    )
    wire = lax.all_to_all(wire.reshape(PAIRS), WAYS, 0, 0, tiled=True)
    wire, grads23 = pl.pallas_call(
        group_kernel,
        grid=(2,),
        in_specs=[SPEC_J, SPEC_W],
        out_specs=[SPEC_J, SPEC_GRAD],
        out_shape=[S(PAIRS, bf16), S((2, 4, 4, 64, BS), bf16)],
        compiler_params=pltpu.CompilerParams(vmem_limit_bytes=VMEM),
        cost_estimate=pl.CostEstimate(flops=6 * ONE, bytes_accessed=10 << 20, transcendentals=1 << 20),
    )(wire, w)
    wire = lax.all_to_all(wire, WAYS, 0, 0, tiled=True)
    sums23 = lax.psum_scatter(grads23.reshape(8, 4, 64, BS), COPIES, scatter_dimension=0, tiled=True)[0]

    acc = pltpu.VMEM((ROWS, BS), f32)
    acts, grads14 = call(
        down_kernel,
        (2,),
        [SPEC_Q, SPEC_X, SPEC_G, SPEC_1, SPEC_4],
        [pl.BlockSpec((8, 2, 64, BS), lambda t, x1: (t, 0, 0, 0)), whole((2, 4, 4, 64, BS))],
        [S((16, 2, 64, BS), bf16), S((2, 4, 4, 64, BS), bf16)],
        4 * ONE,
        8 << 20,
        scratch=[acc, acc],
    )(x1, wire.reshape(WIRE), acts, acts, w, w)

    sums14 = lax.psum_scatter(grads14.reshape(8, 4, 64, BS), COPIES, scatter_dimension=0, tiled=True)[0]
    acts = lax.all_to_all(acts.reshape(32, 64, BS), FAR, 0, 0, tiled=True).reshape(SLOTS)
    g_in, out = call(
        unpack_kernel,
        (4,),
        [
            pl.BlockSpec((1, 1, 2, 2, 64, BS), lambda z, zh: (z, zh[0], 0, 0, 0, 0)),
            pl.BlockSpec((1, 1, 2, 2, 64, BS), lambda z, zh: (z, 1 - zh[0], 0, 0, 0, 0)),
        ],
        [SPEC_T, SPEC_T],
        [S((512, 512), bf16), S((512, 512), bf16)],
        0,
        2 << 20,
    )(zh, acts, acts)
    sums = lax.all_to_all(jnp.concatenate([sums14, sums23], axis=1), SIDE, 0, 0, tiled=True)
    sum1, sum2, sum3, sum4 = call(
        unpack_weights_kernel, (1,), [whole((4, 128, BS))], SPEC_FACTORS, FACTORS, 0, 1 << 20
    )(zh, sums)
    return out, g_in, sum1, sum2, sum3, sum4


def solution(mesh):
    fine = Mesh(mesh.devices.reshape(4, 2, 2, 2, 4, 2), AXES)
    dp, tensor = ("zl", "x1", "x0"), ("zh", "y", "c")
    acts, weights = P(dp, tensor), P(tensor, dp, None)
    return jax.shard_map(
        body,
        mesh=fine,
        in_specs=(acts, acts, weights, weights, weights, weights),
        out_specs=(acts, acts, weights, weights, weights, weights),
        check_vma=False,
    )
```

```python
import jax
import jax.numpy as jnp
from jax import lax
from jax.experimental import pallas as pl
from jax.experimental.pallas import tpu as pltpu
from jax.sharding import Mesh
from jax.sharding import PartitionSpec as P

BS = 256
NA = 32
RR = 8
ROWS = 1024
HALF = 512
AXES = ("zl", "x1", "x0", "zh", "y", "c")
WAYS = ("x1", "y", "c", "x0")
COPIES = ("zh", "zl")
SIDE = ("x1", "x0")
FAR = ("zl", "x1", "x0", "zh")
bf16 = jnp.bfloat16
f32 = jnp.float32
C0 = 0.7978845608028654
C1 = 0.044715
VMEM = 63 * 1024 * 1024 + 512 * 1024
ONE = 2 * 1024 * 1024 * 256
S = jax.ShapeDtypeStruct


def dot(a, b, ca, cb):
    return lax.dot_general(a, b, (((ca,), (cb,)), ((), ())), preferred_element_type=f32)


def pack_kernel(zh_ref, x_ref, g_ref, first_ref, fourth_ref, out_ref):
    zh = zh_ref[0]
    for p in range(2):
        acts = jnp.where(zh == p, x_ref[...], g_ref[...])
        for b in range(2):
            first = jnp.concatenate([first_ref[b, :, q * BS : q * BS + BS] for q in range(4)], axis=0)
            rows = jnp.where(zh == p, first, fourth_ref[b])
            for t in range(2):
                out_ref[0, p, b, t, :64, :] = acts[t * 64 : t * 64 + 64, b * BS : b * BS + BS]
                out_ref[0, p, b, t, 64:, :] = rows


def pack_inner_kernel(x_ref, second_ref, third_ref, *out_refs):
    for d in range(4):
        at = 2 * lax.rem(x_ref[0] + d, 4)
        for m in range(2):
            out_refs[d][m * 16 : 16 + m * 16] = second_ref[at + m]
            out_refs[d][32 + m * 16 : 48 + m * 16] = third_ref[at + m]


def unpack_inner_kernel(x_ref, *refs):
    sum2_ref, sum3_ref = refs[4:]
    for d in range(4):
        at = 2 * lax.rem(x_ref[0] + 4 - d, 4)
        for m in range(2):
            sum2_ref[at + m] = refs[d][m * 16 : 16 + m * 16].astype(f32)
            sum3_ref[at + m] = refs[d][32 + m * 16 : 48 + m * 16].astype(f32)


def arrange_kernel(at_ref, *refs):
    n = len(refs) - 1
    for d in range(n):
        refs[n][lax.rem(at_ref[0] + n - d, n)] = refs[d][...]


def add_kernel(at_ref, *refs):
    total = refs[0][0].astype(f32)
    for ref in refs[1:8]:
        total += ref[...].astype(f32)
    refs[8][...] = total.astype(bf16)


def up_kernel(x1_ref, x_ref, g_ref, first_ref, fourth_ref, out_ref):
    first = first_ref[...].reshape(16, 4, 16, BS)
    first = jnp.concatenate([first[:, q].reshape(BS, BS).T for q in range(4)], axis=0)
    mid = dot(first, x_ref[...].reshape(HALF, BS), 1, 1).astype(bf16)
    g_back = dot(fourth_ref[...].reshape(ROWS, BS), g_ref[...].reshape(HALF, BS), 1, 1).astype(bf16)
    for which, values in enumerate((mid, g_back)):
        values = values.reshape(2, 4, 2, 2, 2, 16, HALF)
        for k in range(2):
            for a in range(2):
                out_ref[a, :, :, :, which, k] = values[k, :, :, a]


def group_kernel(in_ref, w_ref, out_ref, grad_ref):
    def rows_of(which, m):
        rows = in_ref[:, which, 0].astype(f32).reshape(NA, 2, RR, ROWS)
        return rows[:, m].reshape(NA * RR, ROWS).astype(bf16)

    def both(values):
        rows = [v.astype(bf16).astype(f32).reshape(NA, 1, RR, ROWS) for v in values]
        return jnp.concatenate(rows, axis=1).reshape(NA, 2 * RR, ROWS).astype(bf16)

    def swapped(values):
        return jnp.concatenate([values[:, 128:], values[:, :128]], axis=1)

    backs, g_mids = [], []
    for m in range(2):
        second = w_ref[0, :, :, m * 16 : m * 16 + 16].reshape(BS, BS)
        third = swapped(w_ref[0, :, :, 32 + m * 16 : 48 + m * 16].reshape(BS, BS))
        mid = rows_of(0, m)
        g_back = rows_of(1, m)
        pre = dot(second.T, mid, 1, 0)
        sq = pre * pre
        th = jnp.tanh(pre * (C0 + (C0 * C1) * sq))
        half = 0.5 * pre
        part = half * th
        hidden = (half + part).astype(bf16)
        backs.append(dot(third.T, hidden, 1, 0))
        slope = (0.5 + 0.5 * th) + (half - part * th) * (C0 + (3.0 * C0 * C1) * sq)
        g_pre = (dot(third, g_back, 1, 0) * slope).astype(bf16)
        g_mids.append(dot(second, g_pre, 1, 0))
        grad_ref[0, :, :, m * 16 : m * 16 + 16] = dot(mid, g_pre, 1, 1).astype(bf16).reshape(4, 4, 16, BS)
        grad3 = swapped(dot(hidden, g_back, 1, 1)).astype(bf16)
        grad_ref[0, :, :, 32 + m * 16 : 48 + m * 16] = grad3.reshape(4, 4, 16, BS)
    out_ref[:, 0, 0] = both(g_mids)
    out_ref[:, 1, 0] = both(backs)


def down_kernel(x1_ref, in_ref, x_ref, g_ref, first_ref, fourth_ref, out_ref, acc1, acc4):
    step = pl.program_id(0)
    x1 = x1_ref[0]
    g_mid, back = (
        jnp.stack(
            [jnp.stack([in_ref[a, :, :, :, which, k] for a in range(2)], axis=2) for k in range(2)], axis=0
        ).reshape(ROWS, HALF)
        for which in range(2)
    )
    first = first_ref[...].reshape(16, 4, 16, BS)
    first = jnp.concatenate([first[:, q].reshape(BS, BS) for q in range(4)], axis=1)
    g_in = dot(first, g_mid, 1, 0)
    out = dot(fourth_ref[...].reshape(ROWS, BS).T, back, 1, 0)
    here = pl.ds(step * 8, 8)
    out_ref[here, x1, :64, :] = g_in.T.astype(bf16).reshape(8, 64, BS)
    out_ref[here, 1 - x1, :64, :] = out.T.astype(bf16).reshape(8, 64, BS)
    grad1 = dot(g_mid, x_ref[...].reshape(HALF, BS), 1, 0)
    grad4 = dot(back, g_ref[...].reshape(HALF, BS), 1, 0)

    @pl.when(step == 0)
    def _():
        acc1[...] = grad1
        acc4[...] = grad4

    @pl.when(step == 1)
    def _():
        for q in range(4):
            rows = slice(q * BS, q * BS + BS)
            grad = (acc1[rows] + grad1[rows]).T.astype(bf16)
            out_ref[:, x1, 64 + q * 16 : 80 + q * 16, :] = grad.reshape(16, 16, BS)
        out_ref[:, 1 - x1, 64:, :] = (acc4[...] + grad4).astype(bf16).reshape(16, 64, BS)


def unpack_kernel(zh_ref, in_ref, out_side_ref, g_in_ref, out_ref, sum1_ref, sum4_ref):
    step = pl.program_id(0)

    @pl.when(step == 0)
    def _():
        sum1_ref[...] = jnp.zeros_like(sum1_ref)
        sum4_ref[...] = jnp.zeros_like(sum4_ref)

    for b in range(2):
        for t in range(2):
            g_in_ref[t * 64 : t * 64 + 64, b * BS : b * BS + BS] = in_ref[0, 0, b, t, :64, :]
            out_ref[t * 64 : t * 64 + 64, b * BS : b * BS + BS] = out_side_ref[0, 0, b, t, :64, :]
        grad1 = in_ref[0, 0, b, 0, 64:, :].astype(f32) + in_ref[0, 0, b, 1, 64:, :].astype(f32)
        for q in range(4):
            sum1_ref[b, :, q * BS : q * BS + BS] += grad1[q * 16 : q * 16 + 16]
        sum4_ref[b] += out_side_ref[0, 0, b, 0, 64:, :].astype(f32) + out_side_ref[0, 0, b, 1, 64:, :].astype(f32)


def call(kernel, grid, in_specs, out_specs, out_shape, flops, nbytes, trans=0, scratch=()):
    return pl.pallas_call(
        kernel,
        grid_spec=pltpu.PrefetchScalarGridSpec(
            num_scalar_prefetch=1,
            grid=grid,
            in_specs=in_specs,
            out_specs=out_specs,
            scratch_shapes=scratch,
        ),
        out_shape=out_shape,
        compiler_params=pltpu.CompilerParams(vmem_limit_bytes=VMEM),
        cost_estimate=pl.CostEstimate(flops=flops, bytes_accessed=nbytes, transcendentals=trans),
    )


SPEC_X = pl.BlockSpec((8, 1, 64, BS), lambda t, x1: (t, x1[0], 0, 0))
SPEC_G = pl.BlockSpec((8, 1, 64, BS), lambda t, x1: (t, 1 - x1[0], 0, 0))
SPEC_1 = pl.BlockSpec((16, 1, 64, BS), lambda t, x1: (0, x1[0], 1, 0))
SPEC_4 = pl.BlockSpec((16, 1, 64, BS), lambda t, x1: (0, 1 - x1[0], 1, 0))
SPEC_Q = pl.BlockSpec((2, 4, 2, 2, 2, 2, 16, HALF), lambda t, x1: (0, 0, 0, 0, 0, 0, 0, t))
SPEC_J = pl.BlockSpec((NA, 2, 1, 16, ROWS), lambda k: (0, 0, k, 0, 0))
SPEC_W = pl.BlockSpec((1, 4, 4, 64, BS), lambda k: (k, 0, 0, 0, 0))
SPEC_T = pl.BlockSpec((128, 512), lambda z, zh: (z, 0))
WIRE = (2, 4, 2, 2, 2, 2, 16, ROWS)
PAIRS = (NA, 2, 2, 16, ROWS)


def whole(shape):
    return pl.BlockSpec(shape, lambda *_: (0,) * len(shape))


SLOTS = (4, 2, 2, 2, 128, BS)
PIECE = S((64, BS), bf16)
PIECES = S((4, 64, BS), bf16)
INNER = S((8, 16, BS), f32)


def along_x(values, d):
    return lax.ppermute(values, SIDE, [(i, (i + d) % 4) for i in range(4)])


def along_z(values, d):
    place = [z % 4 * 2 + z // 4 for z in range(8)]
    return lax.ppermute(values, ("zl", "zh"), [(place[z], place[(z + d) % 8]) for z in range(8)])


def body(tokens, cotangent, w_first, w_second, w_third, w_fourth):
    x1, zh = (lax.axis_index(n).astype(jnp.int32).reshape(1) for n in ("x1", "zh"))
    at_x, at_z = (lax.axis_index(n).astype(jnp.int32).reshape(1) for n in (SIDE, COPIES))
    inner = call(
        pack_inner_kernel, (1,), [whole((8, 16, BS))] * 2, [whole(PIECE.shape)] * 4, [PIECE] * 4, 0, 1 << 18
    )(at_x, w_second, w_third)
    inner = [inner[0]] + [along_x(inner[d], d) for d in (1, 2, 3)]
    inner = call(arrange_kernel, (1,), [whole(PIECE.shape)] * 4, whole(PIECES.shape), PIECES, 0, 1 << 18)(at_x, *inner)

    outer = call(
        pack_kernel,
        (4,),
        [SPEC_T, SPEC_T, whole((2, 16, 1024)), whole((2, 64, BS))],
        pl.BlockSpec((1, 2, 2, 2, 128, BS), lambda z, zh: (z, 0, 0, 0, 0, 0)),
        S(SLOTS, bf16),
        0,
        3 << 20,
    )(zh, tokens, cotangent, w_first, w_fourth)
    outer = lax.all_to_all(outer.reshape(32, 128, BS), FAR, 0, 0, tiled=True).reshape(16, 2, 128, BS)
    outer, inner = lax.optimization_barrier((outer, inner))

    wire = call(up_kernel, (2,), [SPEC_X, SPEC_G, SPEC_1, SPEC_4], SPEC_Q, S(WIRE, bf16), 2 * ONE, 6 << 20)(
        x1, outer, outer, outer, outer
    )
    wire, inner = lax.optimization_barrier((wire, inner))
    inner = [inner] + [along_z(inner, d) for d in range(1, 8)]
    inner = call(
        arrange_kernel, (1,), [whole(PIECES.shape)] * 8, whole((8, 4, 64, BS)), S((8, 4, 64, BS), bf16), 0, 2 << 20
    )(at_z, *inner)
    wire = lax.all_to_all(wire.reshape(PAIRS), WAYS, 0, 0, tiled=True)
    wire, grads = pl.pallas_call(
        group_kernel,
        grid=(2,),
        in_specs=[SPEC_J, SPEC_W],
        out_specs=[SPEC_J, SPEC_W],
        out_shape=[S(PAIRS, bf16), S((2, 4, 4, 64, BS), bf16)],
        compiler_params=pltpu.CompilerParams(vmem_limit_bytes=VMEM),
        cost_estimate=pl.CostEstimate(flops=6 * ONE, bytes_accessed=10 << 20, transcendentals=1 << 20),
    )(wire, inner.reshape(2, 4, 4, 64, BS))
    wire = lax.all_to_all(wire, WAYS, 0, 0, tiled=True)
    grads = grads.reshape(8, 4, 64, BS)
    sums = [
        along_z(lax.dynamic_index_in_dim(grads, lax.rem(at_z[0] + d, 8), keepdims=False), d) for d in range(1, 8)
    ]
    sums = call(
        add_kernel,
        (1,),
        [pl.BlockSpec((1, 4, 64, BS), lambda i, z: (z[0], 0, 0, 0))] + [whole(PIECES.shape)] * 7,
        whole(PIECES.shape),
        PIECES,
        1 << 20,
        2 << 20,
    )(at_z, grads, *sums)
    wire, sums = lax.optimization_barrier((wire, sums))

    acc = pltpu.VMEM((ROWS, BS), f32)
    outer = call(
        down_kernel,
        (2,),
        [SPEC_Q, SPEC_X, SPEC_G, SPEC_1, SPEC_4],
        whole((16, 2, 128, BS)),
        S((16, 2, 128, BS), bf16),
        4 * ONE,
        8 << 20,
        scratch=[acc, acc],
    )(x1, wire.reshape(WIRE), outer, outer, outer, outer)

    outer, sums = lax.optimization_barrier((outer, sums))
    sums = [lax.dynamic_index_in_dim(sums, lax.rem(at_x[0] + d, 4), keepdims=False) for d in range(4)]
    sums = [sums[0]] + [along_x(sums[d], d) for d in (1, 2, 3)]
    sum2, sum3 = call(
        unpack_inner_kernel, (1,), [whole(PIECE.shape)] * 4, [whole(INNER.shape)] * 2, [INNER] * 2, 0, 1 << 19
    )(at_x, *sums)
    outer = lax.all_to_all(outer.reshape(32, 128, BS), FAR, 0, 0, tiled=True).reshape(SLOTS)
    outer, sum2, sum3 = lax.optimization_barrier((outer, sum2, sum3))
    g_in, out, sum1, sum4 = call(
        unpack_kernel,
        (4,),
        [
            pl.BlockSpec((1, 1, 2, 2, 128, BS), lambda z, zh: (z, zh[0], 0, 0, 0, 0)),
            pl.BlockSpec((1, 1, 2, 2, 128, BS), lambda z, zh: (z, 1 - zh[0], 0, 0, 0, 0)),
        ],
        [SPEC_T, SPEC_T, whole((2, 16, 1024)), whole((2, 64, BS))],
        [S((512, 512), bf16), S((512, 512), bf16), S((2, 16, 1024), f32), S((2, 64, BS), f32)],
        1 << 20,
        4 << 20,
    )(zh, outer, outer)
    return out, g_in, sum1, sum2, sum3, sum4


def solution(mesh):
    fine = Mesh(mesh.devices.reshape(4, 2, 2, 2, 4, 2), AXES)
    dp, tensor = ("zl", "x1", "x0"), ("zh", "y", "c")
    acts, weights = P(dp, tensor), P(tensor, dp, None)
    return jax.shard_map(
        body,
        mesh=fine,
        in_specs=(acts, acts, weights, weights, weights, weights),
        out_specs=(acts, acts, weights, weights, weights, weights),
        check_vma=False,
    )
```

```python
import jax
import jax.numpy as jnp
from jax import lax
from jax.experimental import pallas as pl
from jax.experimental.pallas import tpu as pltpu
from jax.sharding import Mesh
from jax.sharding import PartitionSpec as P

BS = 256
NA = 32
RR = 8
ROWS = 1024
HALF = 512
AXES = ("zl", "x1", "x0", "zh", "y", "c")
WAYS = ("x1", "y", "c", "x0")
COPIES = ("zh", "zl")
SIDE = ("x1", "x0")
FAR = ("zl", "x1", "x0", "zh")
bf16 = jnp.bfloat16
f32 = jnp.float32
C0 = 0.7978845608028654
C1 = 0.044715
VMEM = 63 * 1024 * 1024 + 512 * 1024
ONE = 2 * 1024 * 1024 * 256
S = jax.ShapeDtypeStruct


def dot(a, b, ca, cb):
    return lax.dot_general(a, b, (((ca,), (cb,)), ((), ())), preferred_element_type=f32)


def pack_kernel(zh_ref, x_ref, g_ref, first_ref, fourth_ref, out_ref):
    zh = zh_ref[0]
    for p in range(2):
        acts = jnp.where(zh == p, x_ref[...], g_ref[...])
        for b in range(2):
            first = jnp.concatenate([first_ref[b, :, q * BS : q * BS + BS] for q in range(4)], axis=0)
            rows = jnp.where(zh == p, first, fourth_ref[b])
            for z in range(2):
                for t in range(2):
                    at = z * 128 + t * 64
                    out_ref[z, p, b, t, :64, :] = acts[at : at + 64, b * BS : b * BS + BS]
                    out_ref[z, p, b, t, 64:, :] = rows


def pack_inner_kernel(x_ref, second_ref, third_ref, *out_refs):
    for d in range(4):
        at = 2 * lax.rem(x_ref[0] + d, 4)
        for m in range(2):
            out_refs[d][m * 16 : 16 + m * 16] = second_ref[at + m]
            out_refs[d][32 + m * 16 : 48 + m * 16] = third_ref[at + m]


def unpack_inner_kernel(x_ref, *refs):
    sum2_ref, sum3_ref = refs[4:]
    for d in range(4):
        at = 2 * lax.rem(x_ref[0] + 4 - d, 4)
        for m in range(2):
            sum2_ref[at + m] = refs[d][m * 16 : 16 + m * 16].astype(f32)
            sum3_ref[at + m] = refs[d][32 + m * 16 : 48 + m * 16].astype(f32)


def arrange_kernel(at_ref, *refs):
    n = len(refs) - 1
    for d in range(n):
        refs[n][lax.rem(at_ref[0] + n - d, n)] = refs[d][...]


def add_kernel(at_ref, *refs):
    total = refs[0][0].astype(f32)
    for ref in refs[1:8]:
        total += ref[...].astype(f32)
    refs[8][...] = total.astype(bf16)


def up_kernel(x1_ref, x_ref, g_ref, first_ref, fourth_ref, out_ref):
    first = first_ref[...].reshape(16, 4, 16, BS)
    first = jnp.concatenate([first[:, q].reshape(BS, BS).T for q in range(4)], axis=0)
    mid = dot(first, x_ref[...].reshape(HALF, BS), 1, 1).astype(bf16)
    g_back = dot(fourth_ref[...].reshape(ROWS, BS), g_ref[...].reshape(HALF, BS), 1, 1).astype(bf16)
    for which, values in enumerate((mid, g_back)):
        values = values.reshape(2, 4, 2, 2, 2, 16, HALF)
        for k in range(2):
            for a in range(2):
                out_ref[a, :, :, :, which, k] = values[k, :, :, a]


def group_kernel(in_ref, w_ref, out_ref, grad_ref):
    def rows_of(which, m):
        rows = in_ref[:, which, 0].astype(f32).reshape(NA, 2, RR, ROWS)
        return rows[:, m].reshape(NA * RR, ROWS).astype(bf16)

    def both(values):
        rows = [v.astype(bf16).astype(f32).reshape(NA, 1, RR, ROWS) for v in values]
        return jnp.concatenate(rows, axis=1).reshape(NA, 2 * RR, ROWS).astype(bf16)

    def swapped(values):
        return jnp.concatenate([values[:, 128:], values[:, :128]], axis=1)

    backs, g_mids = [], []
    for m in range(2):
        second = w_ref[0, :, :, m * 16 : m * 16 + 16].reshape(BS, BS)
        third = swapped(w_ref[0, :, :, 32 + m * 16 : 48 + m * 16].reshape(BS, BS))
        mid = rows_of(0, m)
        g_back = rows_of(1, m)
        pre = dot(second.T, mid, 1, 0)
        sq = pre * pre
        th = jnp.tanh(pre * (C0 + (C0 * C1) * sq))
        half = 0.5 * pre
        part = half * th
        hidden = (half + part).astype(bf16)
        backs.append(dot(third.T, hidden, 1, 0))
        slope = (0.5 + 0.5 * th) + (half - part * th) * (C0 + (3.0 * C0 * C1) * sq)
        g_pre = (dot(third, g_back, 1, 0) * slope).astype(bf16)
        g_mids.append(dot(second, g_pre, 1, 0))
        grad_ref[0, :, :, m * 16 : m * 16 + 16] = dot(mid, g_pre, 1, 1).astype(bf16).reshape(4, 4, 16, BS)
        grad3 = swapped(dot(hidden, g_back, 1, 1)).astype(bf16)
        grad_ref[0, :, :, 32 + m * 16 : 48 + m * 16] = grad3.reshape(4, 4, 16, BS)
    out_ref[:, 0, 0] = both(g_mids)
    out_ref[:, 1, 0] = both(backs)


def down_kernel(x1_ref, in_ref, x_ref, g_ref, first_ref, fourth_ref, out_ref, acc1, acc4):
    step = pl.program_id(0)
    x1 = x1_ref[0]
    g_mid, back = (
        jnp.stack(
            [jnp.stack([in_ref[a, :, :, :, which, k] for a in range(2)], axis=2) for k in range(2)], axis=0
        ).reshape(ROWS, HALF)
        for which in range(2)
    )
    first = first_ref[...].reshape(16, 4, 16, BS)
    first = jnp.concatenate([first[:, q].reshape(BS, BS) for q in range(4)], axis=1)
    g_in = dot(first, g_mid, 1, 0)
    out = dot(fourth_ref[...].reshape(ROWS, BS).T, back, 1, 0)
    here = pl.ds(step * 8, 8)
    out_ref[here, x1, :64, :] = g_in.T.astype(bf16).reshape(8, 64, BS)
    out_ref[here, 1 - x1, :64, :] = out.T.astype(bf16).reshape(8, 64, BS)
    grad1 = dot(g_mid, x_ref[...].reshape(HALF, BS), 1, 0)
    grad4 = dot(back, g_ref[...].reshape(HALF, BS), 1, 0)

    @pl.when(step == 0)
    def _():
        acc1[...] = grad1
        acc4[...] = grad4

    @pl.when(step == 1)
    def _():
        for q in range(4):
            rows = slice(q * BS, q * BS + BS)
            grad = (acc1[rows] + grad1[rows]).T.astype(bf16)
            out_ref[:, x1, 64 + q * 16 : 80 + q * 16, :] = grad.reshape(16, 16, BS)
        out_ref[:, 1 - x1, 64:, :] = (acc4[...] + grad4).astype(bf16).reshape(16, 64, BS)


def unpack_kernel(zh_ref, in_ref, out_side_ref, g_in_ref, out_ref, sum1_ref, sum4_ref):
    step = pl.program_id(0)

    @pl.when(step == 0)
    def _():
        sum1_ref[...] = jnp.zeros_like(sum1_ref)
        sum4_ref[...] = jnp.zeros_like(sum4_ref)

    for b in range(2):
        grad1, grad4 = jnp.zeros((64, BS), f32), jnp.zeros((64, BS), f32)
        for z in range(2):
            for t in range(2):
                at = z * 128 + t * 64
                g_in_ref[at : at + 64, b * BS : b * BS + BS] = in_ref[z, 0, b, t, :64, :]
                out_ref[at : at + 64, b * BS : b * BS + BS] = out_side_ref[z, 0, b, t, :64, :]
                grad1 += in_ref[z, 0, b, t, 64:, :].astype(f32)
                grad4 += out_side_ref[z, 0, b, t, 64:, :].astype(f32)
        for q in range(4):
            sum1_ref[b, :, q * BS : q * BS + BS] += grad1[q * 16 : q * 16 + 16]
        sum4_ref[b] += grad4


def call(kernel, grid, in_specs, out_specs, out_shape, flops, nbytes, trans=0, scratch=()):
    return pl.pallas_call(
        kernel,
        grid_spec=pltpu.PrefetchScalarGridSpec(
            num_scalar_prefetch=1,
            grid=grid,
            in_specs=in_specs,
            out_specs=out_specs,
            scratch_shapes=scratch,
        ),
        out_shape=out_shape,
        compiler_params=pltpu.CompilerParams(vmem_limit_bytes=VMEM),
        cost_estimate=pl.CostEstimate(flops=flops, bytes_accessed=nbytes, transcendentals=trans),
    )


SPEC_X = pl.BlockSpec((8, 1, 64, BS), lambda t, x1: (t, x1[0], 0, 0))
SPEC_G = pl.BlockSpec((8, 1, 64, BS), lambda t, x1: (t, 1 - x1[0], 0, 0))
SPEC_1 = pl.BlockSpec((16, 1, 64, BS), lambda t, x1: (0, x1[0], 1, 0))
SPEC_4 = pl.BlockSpec((16, 1, 64, BS), lambda t, x1: (0, 1 - x1[0], 1, 0))
SPEC_Q = pl.BlockSpec((2, 4, 2, 2, 2, 2, 16, HALF), lambda t, x1: (0, 0, 0, 0, 0, 0, 0, t))
SPEC_J = pl.BlockSpec((NA, 2, 1, 16, ROWS), lambda k: (0, 0, k, 0, 0))
SPEC_W = pl.BlockSpec((1, 4, 4, 64, BS), lambda k: (k, 0, 0, 0, 0))
SPEC_T = pl.BlockSpec((256, 512), lambda z, zh: (z, 0))
WIRE = (2, 4, 2, 2, 2, 2, 16, ROWS)
PAIRS = (NA, 2, 2, 16, ROWS)


def whole(shape):
    return pl.BlockSpec(shape, lambda *_: (0,) * len(shape))


SLOTS = (4, 2, 2, 2, 128, BS)
PIECE = S((64, BS), bf16)
PIECES = S((4, 64, BS), bf16)
INNER = S((8, 16, BS), f32)


def along_x(values, d):
    return lax.ppermute(values, SIDE, [(i, (i + d) % 4) for i in range(4)])


def along_z(values, d):
    place = [z % 4 * 2 + z // 4 for z in range(8)]
    return lax.ppermute(values, ("zl", "zh"), [(place[z], place[(z + d) % 8]) for z in range(8)])


def body(tokens, cotangent, w_first, w_second, w_third, w_fourth):
    x1, zh = (lax.axis_index(n).astype(jnp.int32).reshape(1) for n in ("x1", "zh"))
    at_x, at_z = (lax.axis_index(n).astype(jnp.int32).reshape(1) for n in (SIDE, COPIES))
    inner = call(
        pack_inner_kernel, (1,), [whole((8, 16, BS))] * 2, [whole(PIECE.shape)] * 4, [PIECE] * 4, 0, 1 << 18
    )(at_x, w_second, w_third)
    inner = [inner[0]] + [along_x(inner[d], d) for d in (1, 2, 3)]
    inner = call(arrange_kernel, (1,), [whole(PIECE.shape)] * 4, whole(PIECES.shape), PIECES, 0, 1 << 18)(at_x, *inner)

    outer = call(
        pack_kernel,
        (2,),
        [SPEC_T, SPEC_T, whole((2, 16, 1024)), whole((2, 64, BS))],
        pl.BlockSpec((2, 2, 2, 2, 128, BS), lambda z, zh: (z, 0, 0, 0, 0, 0)),
        S(SLOTS, bf16),
        0,
        3 << 20,
    )(zh, tokens, cotangent, w_first, w_fourth)
    outer = lax.all_to_all(outer.reshape(32, 128, BS), FAR, 0, 0, tiled=True).reshape(16, 2, 128, BS)
    outer, inner = lax.optimization_barrier((outer, inner))

    wire = call(up_kernel, (2,), [SPEC_X, SPEC_G, SPEC_1, SPEC_4], SPEC_Q, S(WIRE, bf16), 2 * ONE, 6 << 20)(
        x1, outer, outer, outer, outer
    )
    wire, inner = lax.optimization_barrier((wire, inner))
    inner = [inner] + [along_z(inner, d) for d in range(1, 8)]
    inner = call(
        arrange_kernel, (1,), [whole(PIECES.shape)] * 8, whole((8, 4, 64, BS)), S((8, 4, 64, BS), bf16), 0, 2 << 20
    )(at_z, *inner)
    wire = lax.all_to_all(wire.reshape(PAIRS), WAYS, 0, 0, tiled=True)
    wire, grads = pl.pallas_call(
        group_kernel,
        grid=(2,),
        in_specs=[SPEC_J, SPEC_W],
        out_specs=[SPEC_J, SPEC_W],
        out_shape=[S(PAIRS, bf16), S((2, 4, 4, 64, BS), bf16)],
        compiler_params=pltpu.CompilerParams(vmem_limit_bytes=VMEM),
        cost_estimate=pl.CostEstimate(flops=6 * ONE, bytes_accessed=10 << 20, transcendentals=1 << 20),
    )(wire, inner.reshape(2, 4, 4, 64, BS))
    wire = lax.all_to_all(wire, WAYS, 0, 0, tiled=True)
    grads = grads.reshape(8, 4, 64, BS)
    sums = [
        along_z(lax.dynamic_index_in_dim(grads, lax.rem(at_z[0] + d, 8), keepdims=False), d) for d in range(1, 8)
    ]
    sums = call(
        add_kernel,
        (1,),
        [pl.BlockSpec((1, 4, 64, BS), lambda i, z: (z[0], 0, 0, 0))] + [whole(PIECES.shape)] * 7,
        whole(PIECES.shape),
        PIECES,
        1 << 20,
        2 << 20,
    )(at_z, grads, *sums)
    wire, sums = lax.optimization_barrier((wire, sums))

    acc = pltpu.VMEM((ROWS, BS), f32)
    outer = call(
        down_kernel,
        (2,),
        [SPEC_Q, SPEC_X, SPEC_G, SPEC_1, SPEC_4],
        whole((16, 2, 128, BS)),
        S((16, 2, 128, BS), bf16),
        4 * ONE,
        8 << 20,
        scratch=[acc, acc],
    )(x1, wire.reshape(WIRE), outer, outer, outer, outer)

    outer, sums = lax.optimization_barrier((outer, sums))
    sums = [lax.dynamic_index_in_dim(sums, lax.rem(at_x[0] + d, 4), keepdims=False) for d in range(4)]
    sums = [sums[0]] + [along_x(sums[d], d) for d in (1, 2, 3)]
    sum2, sum3 = call(
        unpack_inner_kernel, (1,), [whole(PIECE.shape)] * 4, [whole(INNER.shape)] * 2, [INNER] * 2, 0, 1 << 19
    )(at_x, *sums)
    outer = lax.all_to_all(outer.reshape(32, 128, BS), FAR, 0, 0, tiled=True).reshape(SLOTS)
    outer, sum2, sum3 = lax.optimization_barrier((outer, sum2, sum3))
    g_in, out, sum1, sum4 = call(
        unpack_kernel,
        (2,),
        [
            pl.BlockSpec((2, 1, 2, 2, 128, BS), lambda z, zh: (z, zh[0], 0, 0, 0, 0)),
            pl.BlockSpec((2, 1, 2, 2, 128, BS), lambda z, zh: (z, 1 - zh[0], 0, 0, 0, 0)),
        ],
        [SPEC_T, SPEC_T, whole((2, 16, 1024)), whole((2, 64, BS))],
        [S((512, 512), bf16), S((512, 512), bf16), S((2, 16, 1024), f32), S((2, 64, BS), f32)],
        1 << 20,
        4 << 20,
    )(zh, outer, outer)
    return out, g_in, sum1, sum2, sum3, sum4


def solution(mesh):
    fine = Mesh(mesh.devices.reshape(4, 2, 2, 2, 4, 2), AXES)
    dp, tensor = ("zl", "x1", "x0"), ("zh", "y", "c")
    acts, weights = P(dp, tensor), P(tensor, dp, None)
    return jax.shard_map(
        body,
        mesh=fine,
        in_specs=(acts, acts, weights, weights, weights, weights),
        out_specs=(acts, acts, weights, weights, weights, weights),
        check_vma=False,
    )
```

```python
import jax
import jax.numpy as jnp
from jax import lax
from jax.experimental import pallas as pl
from jax.experimental.pallas import tpu as pltpu
from jax.sharding import Mesh
from jax.sharding import PartitionSpec as P

BS = 256
NA = 32
RR = 8
ROWS = 1024
HALF = 512
AXES = ("zl", "x1", "x0", "zh", "y", "c")
WAYS = ("x1", "y", "c", "x0")
COPIES = ("zh", "zl")
SIDE = ("x1", "x0")
FAR = ("zl", "x1", "x0", "zh")
bf16 = jnp.bfloat16
f32 = jnp.float32
C0 = 0.7978845608028654
C1 = 0.044715
VMEM = 63 * 1024 * 1024 + 512 * 1024
ONE = 2 * 1024 * 1024 * 256
S = jax.ShapeDtypeStruct


def dot(a, b, ca, cb):
    return lax.dot_general(a, b, (((ca,), (cb,)), ((), ())), preferred_element_type=f32)


def pack_kernel(zh_ref, x_ref, g_ref, first_ref, fourth_ref, out_ref):
    zh = zh_ref[0]
    for p in range(2):
        acts = jnp.where(zh == p, x_ref[...], g_ref[...])
        for b in range(2):
            first = jnp.concatenate([first_ref[b, :, q * BS : q * BS + BS] for q in range(4)], axis=0)
            rows = jnp.where(zh == p, first, fourth_ref[b])
            for z in range(2):
                for t in range(2):
                    at = z * 128 + t * 64
                    out_ref[z, p, b, t, :64, :] = acts[at : at + 64, b * BS : b * BS + BS]
                    out_ref[z, p, b, t, 64:, :] = rows


def pack_inner_kernel(x_ref, second_ref, third_ref, *out_refs):
    for d in range(4):
        at = 2 * lax.rem(x_ref[0] + d, 4)
        for m in range(2):
            out_refs[d][m * 16 : 16 + m * 16] = second_ref[at + m]
            out_refs[d][32 + m * 16 : 48 + m * 16] = third_ref[at + m]


def unpack_inner_kernel(x_ref, *refs):
    sum2_ref, sum3_ref = refs[4:]
    for d in range(4):
        at = 2 * lax.rem(x_ref[0] + 4 - d, 4)
        for m in range(2):
            sum2_ref[at + m] = refs[d][m * 16 : 16 + m * 16].astype(f32)
            sum3_ref[at + m] = refs[d][32 + m * 16 : 48 + m * 16].astype(f32)


def arrange_kernel(at_ref, *refs):
    n = len(refs) - 1
    for d in range(n):
        refs[n][lax.rem(at_ref[0] + n - d, n)] = refs[d][...]


def add_kernel(at_ref, *refs):
    total = refs[0][0].astype(f32)
    for ref in refs[1:8]:
        total += ref[...].astype(f32)
    refs[8][...] = total.astype(bf16)


def up_kernel(x1_ref, x_ref, g_ref, first_ref, fourth_ref, out_ref):
    first = first_ref[...].reshape(16, 4, 16, BS)
    first = jnp.concatenate([first[:, q].reshape(BS, BS).T for q in range(4)], axis=0)
    mid = dot(first, x_ref[...].reshape(HALF, BS), 1, 1).astype(bf16)
    g_back = dot(fourth_ref[...].reshape(ROWS, BS), g_ref[...].reshape(HALF, BS), 1, 1).astype(bf16)
    for which, values in enumerate((mid, g_back)):
        values = values.reshape(2, 4, 2, 2, 2, 16, HALF)
        for k in range(2):
            for a in range(2):
                out_ref[a, :, :, :, which, k] = values[k, :, :, a]


def group_kernel(in_ref, w_ref, out_ref, grad_ref):
    def rows_of(which, m):
        rows = in_ref[:, which, 0].astype(f32).reshape(NA, 2, RR, ROWS)
        return rows[:, m].reshape(NA * RR, ROWS).astype(bf16)

    def both(values):
        rows = [v.astype(bf16).astype(f32).reshape(NA, 1, RR, ROWS) for v in values]
        return jnp.concatenate(rows, axis=1).reshape(NA, 2 * RR, ROWS).astype(bf16)

    def swapped(values):
        return jnp.concatenate([values[:, 128:], values[:, :128]], axis=1)

    backs, g_mids = [], []
    for m in range(2):
        second = w_ref[0, :, :, m * 16 : m * 16 + 16].reshape(BS, BS)
        third = swapped(w_ref[0, :, :, 32 + m * 16 : 48 + m * 16].reshape(BS, BS))
        mid = rows_of(0, m)
        g_back = rows_of(1, m)
        pre = dot(second.T, mid, 1, 0)
        sq = pre * pre
        th = jnp.tanh(pre * (C0 + (C0 * C1) * sq))
        half = 0.5 * pre
        part = half * th
        hidden = (half + part).astype(bf16)
        backs.append(dot(third.T, hidden, 1, 0))
        slope = (0.5 + 0.5 * th) + (half - part * th) * (C0 + (3.0 * C0 * C1) * sq)
        g_pre = (dot(third, g_back, 1, 0) * slope).astype(bf16)
        g_mids.append(dot(second, g_pre, 1, 0))
        grad_ref[0, :, :, m * 16 : m * 16 + 16] = dot(mid, g_pre, 1, 1).astype(bf16).reshape(4, 4, 16, BS)
        grad3 = swapped(dot(hidden, g_back, 1, 1)).astype(bf16)
        grad_ref[0, :, :, 32 + m * 16 : 48 + m * 16] = grad3.reshape(4, 4, 16, BS)
    out_ref[:, 0, 0] = both(g_mids)
    out_ref[:, 1, 0] = both(backs)


def down_kernel(x1_ref, in_ref, x_ref, g_ref, first_ref, fourth_ref, out_ref, acc1, acc4):
    step = pl.program_id(0)
    x1 = x1_ref[0]
    g_mid, back = (
        jnp.stack(
            [jnp.stack([in_ref[a, :, :, :, which, k] for a in range(2)], axis=2) for k in range(2)], axis=0
        ).reshape(ROWS, HALF)
        for which in range(2)
    )
    first = first_ref[...].reshape(16, 4, 16, BS)
    first = jnp.concatenate([first[:, q].reshape(BS, BS) for q in range(4)], axis=1)
    g_in = dot(first, g_mid, 1, 0)
    out = dot(fourth_ref[...].reshape(ROWS, BS).T, back, 1, 0)
    here = pl.ds(step * 8, 8)
    out_ref[here, x1, :64, :] = g_in.T.astype(bf16).reshape(8, 64, BS)
    out_ref[here, 1 - x1, :64, :] = out.T.astype(bf16).reshape(8, 64, BS)
    grad1 = dot(g_mid, x_ref[...].reshape(HALF, BS), 1, 0)
    grad4 = dot(back, g_ref[...].reshape(HALF, BS), 1, 0)

    @pl.when(step == 0)
    def _():
        acc1[...] = grad1
        acc4[...] = grad4

    @pl.when(step == 1)
    def _():
        for q in range(4):
            rows = slice(q * BS, q * BS + BS)
            grad = (acc1[rows] + grad1[rows]).T.astype(bf16)
            out_ref[:, x1, 64 + q * 16 : 80 + q * 16, :] = grad.reshape(16, 16, BS)
        out_ref[:, 1 - x1, 64:, :] = (acc4[...] + grad4).astype(bf16).reshape(16, 64, BS)


def unpack_kernel(zh_ref, in_ref, out_side_ref, g_in_ref, out_ref, sum1_ref, sum4_ref):
    step = pl.program_id(0)

    @pl.when(step == 0)
    def _():
        sum1_ref[...] = jnp.zeros_like(sum1_ref)
        sum4_ref[...] = jnp.zeros_like(sum4_ref)

    for b in range(2):
        grad1, grad4 = jnp.zeros((64, BS), f32), jnp.zeros((64, BS), f32)
        for z in range(2):
            for t in range(2):
                at = z * 128 + t * 64
                g_in_ref[at : at + 64, b * BS : b * BS + BS] = in_ref[z, 0, b, t, :64, :]
                out_ref[at : at + 64, b * BS : b * BS + BS] = out_side_ref[z, 0, b, t, :64, :]
                grad1 += in_ref[z, 0, b, t, 64:, :].astype(f32)
                grad4 += out_side_ref[z, 0, b, t, 64:, :].astype(f32)
        for q in range(4):
            sum1_ref[b, :, q * BS : q * BS + BS] += grad1[q * 16 : q * 16 + 16]
        sum4_ref[b] += grad4


def call(kernel, grid, in_specs, out_specs, out_shape, flops, nbytes, trans=0, scratch=()):
    return pl.pallas_call(
        kernel,
        grid_spec=pltpu.PrefetchScalarGridSpec(
            num_scalar_prefetch=1,
            grid=grid,
            in_specs=in_specs,
            out_specs=out_specs,
            scratch_shapes=scratch,
        ),
        out_shape=out_shape,
        compiler_params=pltpu.CompilerParams(vmem_limit_bytes=VMEM),
        cost_estimate=pl.CostEstimate(flops=flops, bytes_accessed=nbytes, transcendentals=trans),
    )


SPEC_X = pl.BlockSpec((8, 1, 64, BS), lambda t, x1: (t, x1[0], 0, 0))
SPEC_G = pl.BlockSpec((8, 1, 64, BS), lambda t, x1: (t, 1 - x1[0], 0, 0))
SPEC_1 = pl.BlockSpec((16, 1, 64, BS), lambda t, x1: (0, x1[0], 1, 0))
SPEC_4 = pl.BlockSpec((16, 1, 64, BS), lambda t, x1: (0, 1 - x1[0], 1, 0))
SPEC_Q = pl.BlockSpec((2, 4, 2, 2, 2, 2, 16, HALF), lambda t, x1: (0, 0, 0, 0, 0, 0, 0, t))
SPEC_J = pl.BlockSpec((NA, 2, 1, 16, ROWS), lambda k: (0, 0, k, 0, 0))
SPEC_W = pl.BlockSpec((1, 4, 4, 64, BS), lambda k: (k, 0, 0, 0, 0))
SPEC_T = pl.BlockSpec((256, 512), lambda z, zh: (z, 0))
WIRE = (2, 4, 2, 2, 2, 2, 16, ROWS)
PAIRS = (NA, 2, 2, 16, ROWS)


def whole(shape):
    return pl.BlockSpec(shape, lambda *_: (0,) * len(shape))


SLOTS = (4, 2, 2, 2, 128, BS)
PIECE = S((64, BS), bf16)
PIECES = S((4, 64, BS), bf16)
INNER = S((8, 16, BS), f32)


def along_x(values, d):
    return lax.ppermute(values, SIDE, [(i, (i + d) % 4) for i in range(4)])


def along_z(values, d):
    place = [z % 4 * 2 + z // 4 for z in range(8)]
    return lax.ppermute(values, ("zl", "zh"), [(place[z], place[(z + d) % 8]) for z in range(8)])


def body(tokens, cotangent, w_first, w_second, w_third, w_fourth):
    x1, zh = (lax.axis_index(n).astype(jnp.int32).reshape(1) for n in ("x1", "zh"))
    at_x, at_z = (lax.axis_index(n).astype(jnp.int32).reshape(1) for n in (SIDE, COPIES))
    inner = call(
        pack_inner_kernel, (1,), [whole((8, 16, BS))] * 2, [whole(PIECE.shape)] * 4, [PIECE] * 4, 0, 1 << 18
    )(at_x, w_second, w_third)
    inner = [inner[0]] + [along_x(inner[d], d) for d in (1, 2, 3)]
    inner = call(arrange_kernel, (1,), [whole(PIECE.shape)] * 4, whole(PIECES.shape), PIECES, 0, 1 << 18)(at_x, *inner)

    outer = call(
        pack_kernel,
        (2,),
        [SPEC_T, SPEC_T, whole((2, 16, 1024)), whole((2, 64, BS))],
        pl.BlockSpec((2, 2, 2, 2, 128, BS), lambda z, zh: (z, 0, 0, 0, 0, 0)),
        S(SLOTS, bf16),
        0,
        3 << 20,
    )(zh, tokens, cotangent, w_first, w_fourth)
    outer = lax.all_to_all(outer.reshape(32, 128, BS), FAR, 0, 0, tiled=True).reshape(16, 2, 128, BS)
    outer, inner = lax.optimization_barrier((outer, inner))

    wire = call(up_kernel, (2,), [SPEC_X, SPEC_G, SPEC_1, SPEC_4], SPEC_Q, S(WIRE, bf16), 2 * ONE, 6 << 20)(
        x1, outer, outer, outer, outer
    )
    wire, inner = lax.optimization_barrier((wire, inner))
    inner = [inner] + [along_z(inner, d) for d in range(1, 8)]
    inner = call(
        arrange_kernel, (1,), [whole(PIECES.shape)] * 8, whole((8, 4, 64, BS)), S((8, 4, 64, BS), bf16), 0, 2 << 20
    )(at_z, *inner)
    wire = lax.all_to_all(wire.reshape(PAIRS), WAYS, 0, 0, tiled=True)
    wire, grads = pl.pallas_call(
        group_kernel,
        grid=(2,),
        in_specs=[SPEC_J, SPEC_W],
        out_specs=[SPEC_J, SPEC_W],
        out_shape=[S(PAIRS, bf16), S((2, 4, 4, 64, BS), bf16)],
        compiler_params=pltpu.CompilerParams(vmem_limit_bytes=VMEM),
        cost_estimate=pl.CostEstimate(flops=6 * ONE, bytes_accessed=10 << 20, transcendentals=1 << 20),
    )(wire, inner.reshape(2, 4, 4, 64, BS))
    wire = lax.all_to_all(wire, WAYS, 0, 0, tiled=True)
    grads = grads.reshape(8, 4, 64, BS)
    sums = [
        along_z(lax.dynamic_index_in_dim(grads, lax.rem(at_z[0] + d, 8), keepdims=False), d) for d in range(1, 8)
    ]
    sums = call(
        add_kernel,
        (1,),
        [pl.BlockSpec((1, 4, 64, BS), lambda i, z: (z[0], 0, 0, 0))] + [whole(PIECES.shape)] * 7,
        whole(PIECES.shape),
        PIECES,
        1 << 20,
        2 << 20,
    )(at_z, grads, *sums)
    sums = [lax.dynamic_index_in_dim(sums, lax.rem(at_x[0] + d, 4), keepdims=False) for d in range(4)]
    sums = [sums[0]] + [along_x(sums[d], d) for d in (1, 2, 3)]
    wire, sums = lax.optimization_barrier((wire, sums))

    acc = pltpu.VMEM((ROWS, BS), f32)
    outer = call(
        down_kernel,
        (2,),
        [SPEC_Q, SPEC_X, SPEC_G, SPEC_1, SPEC_4],
        whole((16, 2, 128, BS)),
        S((16, 2, 128, BS), bf16),
        4 * ONE,
        8 << 20,
        scratch=[acc, acc],
    )(x1, wire.reshape(WIRE), outer, outer, outer, outer)

    outer, sums = lax.optimization_barrier((outer, sums))
    sum2, sum3 = call(
        unpack_inner_kernel, (1,), [whole(PIECE.shape)] * 4, [whole(INNER.shape)] * 2, [INNER] * 2, 0, 1 << 19
    )(at_x, *sums)
    outer = lax.all_to_all(outer.reshape(32, 128, BS), FAR, 0, 0, tiled=True).reshape(SLOTS)
    outer, sum2, sum3 = lax.optimization_barrier((outer, sum2, sum3))
    g_in, out, sum1, sum4 = call(
        unpack_kernel,
        (2,),
        [
            pl.BlockSpec((2, 1, 2, 2, 128, BS), lambda z, zh: (z, zh[0], 0, 0, 0, 0)),
            pl.BlockSpec((2, 1, 2, 2, 128, BS), lambda z, zh: (z, 1 - zh[0], 0, 0, 0, 0)),
        ],
        [SPEC_T, SPEC_T, whole((2, 16, 1024)), whole((2, 64, BS))],
        [S((512, 512), bf16), S((512, 512), bf16), S((2, 16, 1024), f32), S((2, 64, BS), f32)],
        1 << 20,
        4 << 20,
    )(zh, outer, outer)
    return out, g_in, sum1, sum2, sum3, sum4


def solution(mesh):
    fine = Mesh(mesh.devices.reshape(4, 2, 2, 2, 4, 2), AXES)
    dp, tensor = ("zl", "x1", "x0"), ("zh", "y", "c")
    acts, weights = P(dp, tensor), P(tensor, dp, None)
    return jax.shard_map(
        body,
        mesh=fine,
        in_specs=(acts, acts, weights, weights, weights, weights),
        out_specs=(acts, acts, weights, weights, weights, weights),
        check_vma=False,
    )
```

```python
import jax
import jax.numpy as jnp
from jax import lax
from jax.experimental import pallas as pl
from jax.experimental.pallas import tpu as pltpu
from jax.sharding import Mesh
from jax.sharding import PartitionSpec as P

BS = 256
NA = 32
RR = 8
ROWS = 1024
HALF = 512
AXES = ("zl", "x1", "x0", "zh", "y", "c")
WAYS = ("x1", "y", "c", "x0")
COPIES = ("zh", "zl")
SIDE = ("x1", "x0")
FAR = ("zl", "x1", "x0", "zh")
bf16 = jnp.bfloat16
f32 = jnp.float32
C0 = 0.7978845608028654
C1 = 0.044715
VMEM = 63 * 1024 * 1024 + 512 * 1024
ONE = 2 * 1024 * 1024 * 256
S = jax.ShapeDtypeStruct


def dot(a, b, ca, cb):
    return lax.dot_general(a, b, (((ca,), (cb,)), ((), ())), preferred_element_type=f32)


def pack_kernel(zh_ref, x_ref, g_ref, first_ref, fourth_ref, out_ref):
    zh = zh_ref[0]
    for p in range(2):
        acts = jnp.where(zh == p, x_ref[...], g_ref[...])
        for b in range(2):
            first = jnp.concatenate([first_ref[b, :, q * BS : q * BS + BS] for q in range(4)], axis=0)
            rows = jnp.where(zh == p, first, fourth_ref[b])
            for z in range(2):
                for t in range(2):
                    at = z * 128 + t * 64
                    out_ref[z, p, b, t, :64, :] = acts[at : at + 64, b * BS : b * BS + BS]
                    out_ref[z, p, b, t, 64:, :] = rows


def pack_inner_kernel(x_ref, second_ref, third_ref, *out_refs):
    for d in range(4):
        at = 2 * lax.rem(x_ref[0] + d, 4)
        for m in range(2):
            out_refs[d][m * 16 : 16 + m * 16] = second_ref[at + m]
            out_refs[d][32 + m * 16 : 48 + m * 16] = third_ref[at + m]


def unpack_inner_kernel(x_ref, *refs):
    sum2_ref, sum3_ref = refs[4:]
    for d in range(4):
        at = 2 * lax.rem(x_ref[0] + 4 - d, 4)
        for m in range(2):
            sum2_ref[at + m] = refs[d][m * 16 : 16 + m * 16].astype(f32)
            sum3_ref[at + m] = refs[d][32 + m * 16 : 48 + m * 16].astype(f32)


def arrange_kernel(at_ref, *refs):
    n = len(refs) - 1
    for d in range(n):
        refs[n][lax.rem(at_ref[0] + n - d, n)] = refs[d][...]


def add_kernel(at_ref, *refs):
    total = refs[0][0].astype(f32)
    for ref in refs[1:8]:
        total += ref[...].astype(f32)
    refs[8][...] = total.astype(bf16)


def up_kernel(x1_ref, x_ref, g_ref, first_ref, fourth_ref, out_ref):
    first = first_ref[...].reshape(16, 4, 16, BS)
    first = jnp.concatenate([first[:, q].reshape(BS, BS).T for q in range(4)], axis=0)
    mid = dot(first, x_ref[...].reshape(HALF, BS), 1, 1).astype(bf16)
    g_back = dot(fourth_ref[...].reshape(ROWS, BS), g_ref[...].reshape(HALF, BS), 1, 1).astype(bf16)
    for which, values in enumerate((mid, g_back)):
        values = values.reshape(2, 4, 2, 2, 2, 16, HALF)
        for k in range(2):
            for a in range(2):
                out_ref[a, :, :, :, which, k] = values[k, :, :, a]


def group_kernel(in_ref, w_ref, out_ref, grad_ref):
    def rows_of(which, m):
        rows = in_ref[:, which, 0].astype(f32).reshape(NA, 2, RR, ROWS)
        return rows[:, m].reshape(NA * RR, ROWS).astype(bf16)

    def both(values):
        rows = [v.astype(bf16).astype(f32).reshape(NA, 1, RR, ROWS) for v in values]
        return jnp.concatenate(rows, axis=1).reshape(NA, 2 * RR, ROWS).astype(bf16)

    def swapped(values):
        return jnp.concatenate([values[:, 128:], values[:, :128]], axis=1)

    backs, g_mids = [], []
    for m in range(2):
        second = w_ref[0, :, :, m * 16 : m * 16 + 16].reshape(BS, BS)
        third = swapped(w_ref[0, :, :, 32 + m * 16 : 48 + m * 16].reshape(BS, BS))
        mid = rows_of(0, m)
        g_back = rows_of(1, m)
        pre = dot(second.T, mid, 1, 0)
        sq = pre * pre
        th = jnp.tanh(pre * (C0 + (C0 * C1) * sq))
        half = 0.5 * pre
        part = half * th
        hidden = (half + part).astype(bf16)
        backs.append(dot(third.T, hidden, 1, 0))
        slope = (0.5 + 0.5 * th) + (half - part * th) * (C0 + (3.0 * C0 * C1) * sq)
        g_pre = (dot(third, g_back, 1, 0) * slope).astype(bf16)
        g_mids.append(dot(second, g_pre, 1, 0))
        grad_ref[0, :, :, m * 16 : m * 16 + 16] = dot(mid, g_pre, 1, 1).astype(bf16).reshape(4, 4, 16, BS)
        grad3 = swapped(dot(hidden, g_back, 1, 1)).astype(bf16)
        grad_ref[0, :, :, 32 + m * 16 : 48 + m * 16] = grad3.reshape(4, 4, 16, BS)
    out_ref[:, 0, 0] = both(g_mids)
    out_ref[:, 1, 0] = both(backs)


def down_kernel(x1_ref, in_ref, x_ref, g_ref, first_ref, fourth_ref, out_ref, acc1, acc4):
    step = pl.program_id(0)
    x1 = x1_ref[0]
    g_mid, back = (
        jnp.stack(
            [jnp.stack([in_ref[a, :, :, :, which, k] for a in range(2)], axis=2) for k in range(2)], axis=0
        ).reshape(ROWS, HALF)
        for which in range(2)
    )
    first = first_ref[...].reshape(16, 4, 16, BS)
    first = jnp.concatenate([first[:, q].reshape(BS, BS) for q in range(4)], axis=1)
    g_in = dot(first, g_mid, 1, 0)
    out = dot(fourth_ref[...].reshape(ROWS, BS).T, back, 1, 0)
    here = pl.ds(step * 8, 8)
    out_ref[here, x1, :64, :] = g_in.T.astype(bf16).reshape(8, 64, BS)
    out_ref[here, 1 - x1, :64, :] = out.T.astype(bf16).reshape(8, 64, BS)
    grad1 = dot(g_mid, x_ref[...].reshape(HALF, BS), 1, 0)
    grad4 = dot(back, g_ref[...].reshape(HALF, BS), 1, 0)

    @pl.when(step == 0)
    def _():
        acc1[...] = grad1
        acc4[...] = grad4

    @pl.when(step == 1)
    def _():
        for q in range(4):
            rows = slice(q * BS, q * BS + BS)
            grad = (acc1[rows] + grad1[rows]).T.astype(bf16)
            out_ref[:, x1, 64 + q * 16 : 80 + q * 16, :] = grad.reshape(16, 16, BS)
        out_ref[:, 1 - x1, 64:, :] = (acc4[...] + grad4).astype(bf16).reshape(16, 64, BS)


def unpack_kernel(zh_ref, in_ref, out_side_ref, g_in_ref, out_ref, sum1_ref, sum4_ref):
    step = pl.program_id(0)

    @pl.when(step == 0)
    def _():
        sum1_ref[...] = jnp.zeros_like(sum1_ref)
        sum4_ref[...] = jnp.zeros_like(sum4_ref)

    for b in range(2):
        grad1, grad4 = jnp.zeros((64, BS), f32), jnp.zeros((64, BS), f32)
        for z in range(2):
            for t in range(2):
                at = z * 128 + t * 64
                g_in_ref[at : at + 64, b * BS : b * BS + BS] = in_ref[z, 0, b, t, :64, :]
                out_ref[at : at + 64, b * BS : b * BS + BS] = out_side_ref[z, 0, b, t, :64, :]
                grad1 += in_ref[z, 0, b, t, 64:, :].astype(f32)
                grad4 += out_side_ref[z, 0, b, t, 64:, :].astype(f32)
        for q in range(4):
            sum1_ref[b, :, q * BS : q * BS + BS] += grad1[q * 16 : q * 16 + 16]
        sum4_ref[b] += grad4


def call(kernel, grid, in_specs, out_specs, out_shape, flops, nbytes, trans=0, scratch=()):
    return pl.pallas_call(
        kernel,
        grid_spec=pltpu.PrefetchScalarGridSpec(
            num_scalar_prefetch=1,
            grid=grid,
            in_specs=in_specs,
            out_specs=out_specs,
            scratch_shapes=scratch,
        ),
        out_shape=out_shape,
        compiler_params=pltpu.CompilerParams(vmem_limit_bytes=VMEM),
        cost_estimate=pl.CostEstimate(flops=flops, bytes_accessed=nbytes, transcendentals=trans),
    )


SPEC_X = pl.BlockSpec((8, 1, 64, BS), lambda t, x1: (t, x1[0], 0, 0))
SPEC_G = pl.BlockSpec((8, 1, 64, BS), lambda t, x1: (t, 1 - x1[0], 0, 0))
SPEC_1 = pl.BlockSpec((16, 1, 64, BS), lambda t, x1: (0, x1[0], 1, 0))
SPEC_4 = pl.BlockSpec((16, 1, 64, BS), lambda t, x1: (0, 1 - x1[0], 1, 0))
SPEC_Q = pl.BlockSpec((2, 4, 2, 2, 2, 2, 16, HALF), lambda t, x1: (0, 0, 0, 0, 0, 0, 0, t))
SPEC_J = pl.BlockSpec((NA, 2, 1, 16, ROWS), lambda k: (0, 0, k, 0, 0))
SPEC_W = pl.BlockSpec((1, 4, 4, 64, BS), lambda k: (k, 0, 0, 0, 0))
SPEC_T = pl.BlockSpec((256, 512), lambda z, zh: (z, 0))
WIRE = (2, 4, 2, 2, 2, 2, 16, ROWS)
PAIRS = (NA, 2, 2, 16, ROWS)


def whole(shape):
    return pl.BlockSpec(shape, lambda *_: (0,) * len(shape))


SLOTS = (4, 2, 2, 2, 128, BS)
PIECE = S((64, BS), bf16)
PIECES = S((4, 64, BS), bf16)
INNER = S((8, 16, BS), f32)


def along_x(values, d):
    return lax.ppermute(values, SIDE, [(i, (i + d) % 4) for i in range(4)])


def along_z(values, d):
    place = [z % 4 * 2 + z // 4 for z in range(8)]
    return lax.ppermute(values, ("zl", "zh"), [(place[z], place[(z + d) % 8]) for z in range(8)])


def body(tokens, cotangent, w_first, w_second, w_third, w_fourth):
    x1, zh = (lax.axis_index(n).astype(jnp.int32).reshape(1) for n in ("x1", "zh"))
    at_x, at_z = (lax.axis_index(n).astype(jnp.int32).reshape(1) for n in (SIDE, COPIES))
    inner = call(
        pack_inner_kernel, (1,), [whole((8, 16, BS))] * 2, [whole(PIECE.shape)] * 4, [PIECE] * 4, 0, 1 << 18
    )(at_x, w_second, w_third)
    inner = [inner[0]] + [along_x(inner[d], d) for d in (1, 2, 3)]
    inner = call(arrange_kernel, (1,), [whole(PIECE.shape)] * 4, whole(PIECES.shape), PIECES, 0, 1 << 18)(at_x, *inner)

    outer = call(
        pack_kernel,
        (2,),
        [SPEC_T, SPEC_T, whole((2, 16, 1024)), whole((2, 64, BS))],
        pl.BlockSpec((2, 2, 2, 2, 128, BS), lambda z, zh: (z, 0, 0, 0, 0, 0)),
        S(SLOTS, bf16),
        0,
        3 << 20,
    )(zh, tokens, cotangent, w_first, w_fourth)
    outer = lax.all_to_all(outer.reshape(32, 128, BS), FAR, 0, 0, tiled=True).reshape(16, 2, 128, BS)
    outer, inner = lax.optimization_barrier((outer, inner))

    wire = call(up_kernel, (2,), [SPEC_X, SPEC_G, SPEC_1, SPEC_4], SPEC_Q, S(WIRE, bf16), 2 * ONE, 6 << 20)(
        x1, outer, outer, outer, outer
    )
    wire, inner = lax.optimization_barrier((wire, inner))
    far_first = {d: along_z(inner, d) for d in (4, 3, 5, 2, 6, 1, 7)}
    inner = [inner] + [far_first[d] for d in range(1, 8)]
    inner = call(
        arrange_kernel, (1,), [whole(PIECES.shape)] * 8, whole((8, 4, 64, BS)), S((8, 4, 64, BS), bf16), 0, 2 << 20
    )(at_z, *inner)
    wire = lax.all_to_all(wire.reshape(PAIRS), WAYS, 0, 0, tiled=True)
    wire, grads = pl.pallas_call(
        group_kernel,
        grid=(2,),
        in_specs=[SPEC_J, SPEC_W],
        out_specs=[SPEC_J, SPEC_W],
        out_shape=[S(PAIRS, bf16), S((2, 4, 4, 64, BS), bf16)],
        compiler_params=pltpu.CompilerParams(vmem_limit_bytes=VMEM),
        cost_estimate=pl.CostEstimate(flops=6 * ONE, bytes_accessed=10 << 20, transcendentals=1 << 20),
    )(wire, inner.reshape(2, 4, 4, 64, BS))
    wire = lax.all_to_all(wire, WAYS, 0, 0, tiled=True)
    grads = grads.reshape(8, 4, 64, BS)
    sums = [
        along_z(lax.dynamic_index_in_dim(grads, lax.rem(at_z[0] + d, 8), keepdims=False), d)
        for d in (4, 3, 5, 2, 6, 1, 7)
    ]
    sums = call(
        add_kernel,
        (1,),
        [pl.BlockSpec((1, 4, 64, BS), lambda i, z: (z[0], 0, 0, 0))] + [whole(PIECES.shape)] * 7,
        whole(PIECES.shape),
        PIECES,
        1 << 20,
        2 << 20,
    )(at_z, grads, *sums)
    wire, sums = lax.optimization_barrier((wire, sums))

    acc = pltpu.VMEM((ROWS, BS), f32)
    outer = call(
        down_kernel,
        (2,),
        [SPEC_Q, SPEC_X, SPEC_G, SPEC_1, SPEC_4],
        whole((16, 2, 128, BS)),
        S((16, 2, 128, BS), bf16),
        4 * ONE,
        8 << 20,
        scratch=[acc, acc],
    )(x1, wire.reshape(WIRE), outer, outer, outer, outer)

    outer, sums = lax.optimization_barrier((outer, sums))
    sums = [lax.dynamic_index_in_dim(sums, lax.rem(at_x[0] + d, 4), keepdims=False) for d in range(4)]
    sums = [sums[0]] + [along_x(sums[d], d) for d in (1, 2, 3)]
    sum2, sum3 = call(
        unpack_inner_kernel, (1,), [whole(PIECE.shape)] * 4, [whole(INNER.shape)] * 2, [INNER] * 2, 0, 1 << 19
    )(at_x, *sums)
    outer = lax.all_to_all(outer.reshape(32, 128, BS), FAR, 0, 0, tiled=True).reshape(SLOTS)
    outer, sum2, sum3 = lax.optimization_barrier((outer, sum2, sum3))
    g_in, out, sum1, sum4 = call(
        unpack_kernel,
        (2,),
        [
            pl.BlockSpec((2, 1, 2, 2, 128, BS), lambda z, zh: (z, zh[0], 0, 0, 0, 0)),
            pl.BlockSpec((2, 1, 2, 2, 128, BS), lambda z, zh: (z, 1 - zh[0], 0, 0, 0, 0)),
        ],
        [SPEC_T, SPEC_T, whole((2, 16, 1024)), whole((2, 64, BS))],
        [S((512, 512), bf16), S((512, 512), bf16), S((2, 16, 1024), f32), S((2, 64, BS), f32)],
        1 << 20,
        4 << 20,
    )(zh, outer, outer)
    return out, g_in, sum1, sum2, sum3, sum4


def solution(mesh):
    fine = Mesh(mesh.devices.reshape(4, 2, 2, 2, 4, 2), AXES)
    dp, tensor = ("zl", "x1", "x0"), ("zh", "y", "c")
    acts, weights = P(dp, tensor), P(tensor, dp, None)
    return jax.shard_map(
        body,
        mesh=fine,
        in_specs=(acts, acts, weights, weights, weights, weights),
        out_specs=(acts, acts, weights, weights, weights, weights),
        check_vma=False,
    )
```
